512 devices in a mesh: blk: 32 (over x, z_lo), grp: 16 (over z_hi, y, core).
Axes of the slice: x: 4, y: 4, z: 16 (z_hi: 2, z_lo: 8; z = z_hi * 8 + z_lo), core: 2. Of those that a mesh axis runs over, the one named last changes fastest.
Arguments:
- amplitudes: bfloat16 [128, 2048, 2048], P(None, 'blk', 'grp'), may hold values from -6 to 6
- amplitude_map: int32 [32, 32], P('blk', 'grp'), may hold values 0 or 1
- integrals: bfloat16 [2048, 2048], P('blk'), may hold values from -0.375 to 0.375
- integral_map: int32 [32, 32], P('blk'), may hold values from 0 to 1, as said below
- pair_list: int32 [128, 2], replicated, may hold values from 0 to 127
- occupied_energy: float32 [128], replicated, may hold values from -3 to -0.3
- virtual_energy: float32 [2048], replicated, may hold values from 0.2 to 3
Outputs:
- update: bfloat16 [128, 2048, 2048], P(None, 'blk', 'grp')
The draws below stay inside these ranges and needn't reach their ends.
Inputs may be any that keep to these rules, and one draw needn't show every extreme that they name: `integral_map`: each tile row holds between 2 and 16 nonzero tiles, its diagonal tile among them; some tile row holds exactly 16.
All inputs are finite; a program needn't handle non-finite values. No bound on the sum of `amplitude_map` on one device may be relied on, other than what follows from the above.
Results may differ from the reference program's by a relative error of at most 0.0049.
Values may be sent and summed in bfloat16 or wider, within the bound.
A program may use at most 128 MiB of HBM per device.

```python
import jax
import jax.numpy as jnp
from jax import lax

NV = 2048
TILE = 64
NT = 32
CAP = 16
NOCC = 128
PAIRS = 128


def draw_integral_map(key, part):
    key = jax.random.fold_in(key, 11)
    key_count, key_forced, key_score = jax.random.split(key, 3)
    counts = jax.random.randint(key_count, (NT,), 2, CAP + 1)
    forced = jax.random.randint(key_forced, (), 0, NT)
    positions = jnp.arange(NT, dtype=jnp.int32)
    counts = jnp.where(positions == forced, CAP, counts)
    scores = jax.random.randint(key_score, (NT, NT), 0, 1024) * NT + positions[None, :]
    scores = jnp.where(positions[:, None] == positions[None, :], -1, scores)
    ranks = jnp.argsort(jnp.argsort(scores, axis=1), axis=1)
    return (ranks < counts[:, None]).astype(jnp.int32)


def touch_ends(result, own_key, least, largest):
    dims = result.shape
    place = [jax.random.randint(jax.random.fold_in(own_key, axis), (), 0, dims[axis]) for axis in range(len(dims))]
    result = result.at[tuple(place)].set(least)
    longest = dims.index(max(dims))
    place[longest] = (place[longest] + 1) % dims[longest]
    return result.at[tuple(place)].set(largest)


def level_of(own_key, shape, cuts, smallest, largest):
    gain = 1.0
    for position, shards_of in cuts:
        heights = jax.random.uniform(jax.random.fold_in(jax.random.fold_in(own_key, 6), position), (shards_of,), jnp.float32, smallest / len(cuts), largest / len(cuts))
        gain = gain * jnp.repeat(jnp.exp(heights), shape[position] // shards_of).reshape((-1,) + (1,) * (len(shape) - 1 - position))
    return gain


def bell_draw(key, dims, width, limit, cuts=(), kind=jnp.bfloat16):
    entries = jax.random.normal(key, dims, jnp.float32) * width
    if len(cuts) > 0:
        entries = level_of(key, dims, cuts, -0.22, 0.18) * entries
    return jnp.clip(entries, min=-limit, max=limit).astype(kind)


def setup_inputs(seed: int = 0) -> dict:
    splits = jax.random.split(jax.random.key(seed), 8)
    amplitudes = bell_draw(splits[0], (PAIRS, NV, NV), 1.0, 6.0, ((1, 32), (2, 16)))
    amplitude_map = touch_ends((jax.random.randint(splits[1], (NT, NT), 0, 4) < 3).astype(jnp.int32), jax.random.fold_in(splits[1], 1), 0, 1)
    integrals = bell_draw(splits[2], (NV, NV), (NV // 8) ** -0.5, 0.375, ((0, 32),))
    integral_map = draw_integral_map(jax.random.fold_in(splits[7], 71), 0)
    pair_list = touch_ends(jax.random.randint(splits[4], (PAIRS, 2), 0, NOCC), jax.random.fold_in(splits[4], 1), 0, NOCC - 1).astype(jnp.int32)
    occupied_energy = jnp.clip(jax.random.uniform(splits[5], (NOCC,), jnp.float32, -3.0, -0.3), -3.0, -0.3)
    virtual_energy = jnp.clip(jax.random.uniform(splits[6], (NV,), jnp.float32, 0.2, 3.0), 0.2, 3.0)
    return dict(amplitudes=amplitudes, amplitude_map=amplitude_map, integrals=integrals, integral_map=integral_map, pair_list=pair_list, occupied_energy=occupied_energy, virtual_energy=virtual_energy)


def reference(amplitudes, amplitude_map, integrals, integral_map, pair_list, occupied_energy, virtual_energy):
    amp_mask = jnp.repeat(jnp.repeat(amplitude_map, TILE, axis=0), TILE, axis=1).astype(jnp.bfloat16)
    int_mask = jnp.repeat(jnp.repeat(integral_map, TILE, axis=0), TILE, axis=1).astype(jnp.bfloat16)
    masked_int = integrals * int_mask
    shifts = occupied_energy[pair_list[:, 0]] + occupied_energy[pair_list[:, 1]]
    virt_sum = virtual_energy[:, None] + virtual_energy[None, :]

    def one_pair(items):
        block, shift = items
        masked_amp = block * amp_mask
        ladder = lax.dot_general(masked_amp, masked_int, (((1,), (1,)), ((), ())), preferred_element_type=jnp.float32).astype(jnp.bfloat16)
        denominator = virt_sum - shift
        return (ladder.astype(jnp.float32) / denominator).astype(jnp.bfloat16)

    return lax.map(one_pair, (amplitudes, shifts))
```

```python
import jax
import jax.numpy as jnp
from jax import lax
from jax.experimental import pallas as pl
from jax.experimental.pallas import tpu as pltpu
from jax.sharding import PartitionSpec as P

MESH = pl.DeviceIdType.MESH
TILE = 64
NX, NZ, NZL, NJ, NY, NC = 4, 16, 8, 8, 4, 2
CHUNKS = 16
AHEAD = 3
GROUP = 4


def drain(ref, sem):
    pltpu.make_async_copy(ref, ref, sem).wait()


def kernel(
    amp_ref,
    amp_map_ref,
    int_ref,
    int_map_ref,
    pair_ref,
    occ_ref,
    ve_smem,
    ve_row,
    out_ref,
    masked,
    ybuf,
    relay,
    zbuf,
    cbuf,
    bsend,
    bline,
    bfull,
    own_acc,
    erow,
    y_send,
    y_recv,
    z_send,
    z_recv,
    f_send,
    f_recv,
    c_send,
    c_recv,
    own_sem,
    bz_send,
    bz_recv,
    bx_send,
    bx_recv,
    by_send,
    by_recv,
    bc_send,
    bc_recv,
    in_sem,
):
    b = lax.axis_index("blk")
    g = lax.axis_index("grp")
    x, zl = b // NZL, b % NZL
    h, j = g // NJ, g % NJ
    y, c = j // NC, j % NC
    z = h * NZL + zl
    pairs = amp_ref.shape[0] // NJ
    q = pairs // CHUNKS
    half_cols = NJ * 128

    def at_z(zz):
        zz = (zz + NZ) % NZ
        return (x * NZL + zz % NZL, (zz // NZL) * NJ + j)

    def at_j(jj):
        return (b, h * NJ + jj)

    def at_x(xx):
        return (xx * NZL + zl, g)

    peers = [at_z(z + d) for d in (1, 2, 3, 4, -1, -2, -3, -4)]
    peers += [at_j((j + d) % NJ) for d in range(1, NJ)]
    peers += [at_x((x + d) % NX) for d in range(1, NX)]
    barrier = pltpu.get_barrier_semaphore()
    for peer in peers:
        pl.semaphore_signal(barrier, inc=1, device_id=peer, device_id_type=MESH)

    loads = [
        pltpu.make_async_copy(amp_ref, masked, in_sem.at[0]),
        pltpu.make_async_copy(
            int_ref.at[:, pl.ds(pl.multiple_of(j * 256, 128), 256)], bsend, in_sem.at[1]
        ),
    ]
    for load in loads:
        load.start()

    @pl.loop(0, TILE)
    def _(r):
        erow[pl.ds(r, 1), :] = jnp.full((1, 128), ve_smem[b * TILE + r], jnp.float32)

    lane = lax.broadcasted_iota(jnp.int32, (1, 128), 1)
    keep0 = amp_map_ref[0, 0].astype(jnp.float32)
    keep1 = amp_map_ref[0, 1].astype(jnp.float32)
    amp_mask = jnp.where(lane < TILE, keep0, keep1).astype(jnp.bfloat16)

    loads[0].wait()

    @pl.loop(0, NJ * pairs)
    def _(p):
        masked[p] = masked[p] * amp_mask

    ybuf[:, j] = masked[pl.ds(j * pairs, pairs)].reshape(CHUNKS, q, TILE, 128)
    loads[1].wait()
    for half in range(2):
        tile = 4 * j + 2 * half
        keep0 = int_map_ref[0, tile].astype(jnp.float32)
        keep1 = int_map_ref[0, tile + 1].astype(jnp.float32)
        int_mask = jnp.where(lane < TILE, keep0, keep1).astype(jnp.bfloat16)
        cols = slice(half * 128, half * 128 + 128)
        bsend[:, cols] = bsend[:, cols] * int_mask

    pl.semaphore_wait(barrier, len(peers))

    def send_chunk(k):
        for d in range(1, NJ):
            jj = (j + d) % NJ
            pltpu.make_async_remote_copy(
                src_ref=masked.at[pl.ds(jj * pairs + k * q, q)],
                dst_ref=ybuf.at[k, j],
                send_sem=y_send.at[k],
                recv_sem=y_recv.at[k],
                device_id=at_j(jj),
                device_id_type=MESH,
            ).start()

    send_chunk(0)

    in_half = x // 2 == h
    for i, d in enumerate((1, 2, 3, 4, -1, -2, -3)):
        zz = (z + d + NZ) % NZ

        @pl.when(zz // NZL == x // 2)
        def _():
            pltpu.make_async_remote_copy(
                src_ref=bsend,
                dst_ref=bline.at[zl],
                send_sem=bz_send.at[i],
                recv_sem=bz_recv,
                device_id=at_z(zz),
                device_id_type=MESH,
            ).start()

    for k in range(1, AHEAD):
        send_chunk(k)
    bline[zl] = bsend[...]

    def legs(k, first):
        src, dst = (ybuf, relay) if first else (relay, zbuf)
        ssem, rsem = (z_send, z_recv) if first else (f_send, f_recv)
        return [
            pltpu.make_async_remote_copy(
                src_ref=src.at[k, pl.ds(4 * way, 4)],
                dst_ref=dst.at[k, pl.ds(4 * way, 4)],
                send_sem=ssem.at[k, way],
                recv_sem=rsem.at[k, way],
                device_id=at_z(z + (4 if way == 0 else -4)),
                device_id_type=MESH,
            )
            for way in range(2)
        ]

    def b_along_x():
        @pl.when(in_half)
        def _():
            drain(bline.at[pl.ds(0, NZL - 1)], bz_recv)
            bfull[y, c, x % 2] = bline[...].reshape(NZL * TILE, 256).T
            for d in range(1, NX):
                pltpu.make_async_remote_copy(
                    src_ref=bfull.at[y, c, x % 2],
                    dst_ref=bfull.at[y, c, x % 2],
                    send_sem=bx_send.at[d - 1],
                    recv_sem=bx_recv.at[x % 2],
                    device_id=at_x((x + d) % NX),
                    device_id_type=MESH,
                ).start()

    def b_along_y():
        for xx in range(2):

            @pl.when(x != 2 * h + xx)
            def _():
                drain(bfull.at[y, c, xx], bx_recv.at[xx])

        for d in range(1, NY):
            pltpu.make_async_remote_copy(
                src_ref=bfull.at[y, c],
                dst_ref=bfull.at[y, c],
                send_sem=by_send.at[d - 1],
                recv_sem=by_recv.at[y],
                device_id=at_j(((y + d) % NY) * NC + c),
                device_id_type=MESH,
            ).start()

    def b_core():
        for d in range(1, NY):
            yy = (y + d) % NY
            drain(bfull.at[yy, c], by_recv.at[yy])
        return b_core_copies()

    def b_core_copies():
        return [
            pltpu.make_async_remote_copy(
                src_ref=bfull.at[yy, c],
                dst_ref=bfull.at[yy, c],
                send_sem=bc_send.at[yy],
                recv_sem=bc_recv.at[yy],
                device_id=at_j(y * NC + 1 - c),
                device_id_type=MESH,
            )
            for yy in range(NY)
        ]

    def weights(hh, i, n):
        cols = pl.ds(pl.multiple_of((n % 2) * 256, 256), 256)
        return bfull[2 * hh + i // 2, i % 2, n // 2, :, cols]

    def rows_of(buf, first, count, i):
        blocks = [
            buf[pl.ds(first, count), 2 * i + e].reshape(count * q * TILE, 128) for e in range(2)
        ]
        return jnp.concatenate(blocks, axis=1)

    def own_half(group):
        @pl.loop(0, 4)
        def _(n):
            acc = jnp.zeros((GROUP * q * TILE, 256), jnp.float32)
            for i in range(4):
                acc += jnp.dot(
                    rows_of(ybuf, group * GROUP, GROUP, i),
                    weights(h, i, n),
                    preferred_element_type=jnp.float32,
                )
            own_acc[n, pl.ds(group * GROUP, GROUP)] = acc.reshape(GROUP, q * TILE, 256)

    def compute(k):
        @pl.loop(0, 4)
        def _(n):
            acc = own_acc[n, k]
            for i in range(4):
                acc += jnp.dot(
                    rows_of(zbuf, k, 1, i),
                    weights(1 - h, i, n),
                    preferred_element_type=jnp.float32,
                )
            ladder = acc.astype(jnp.bfloat16).astype(jnp.float32)
            for e in range(2):
                start = pl.multiple_of(h * half_cols + n * 256 + e * 128, 128)
                virt = erow[...] + ve_row[:, pl.ds(start, 128)]
                for p in range(q):
                    pair = j * pairs + k * q + p
                    shift = occ_ref[pair_ref[0, pair]] + occ_ref[pair_ref[1, pair]]
                    block = ladder[p * TILE : (p + 1) * TILE, e * 128 : (e + 1) * 128]
                    cbuf[k, 2 * n + e, p] = (block / (virt - shift)).astype(jnp.bfloat16)

        for d in range(1, NJ):
            jj = (j + d) % NJ
            pltpu.make_async_remote_copy(
                src_ref=cbuf.at[k, jj],
                dst_ref=out_ref.at[pl.ds(j * pairs + k * q, q)],
                send_sem=c_send.at[k],
                recv_sem=c_recv,
                device_id=at_j(jj),
                device_id_type=MESH,
            ).start()
        own_copy(k).start()

    def own_copy(k):
        return pltpu.make_async_copy(
            cbuf.at[k, j], out_ref.at[pl.ds(j * pairs + k * q, q)], own_sem.at[k]
        )

    lag1, lag2 = 2, 4

    @pl.loop(0, CHUNKS + lag2)
    def _(t):
        @pl.when(t + AHEAD < CHUNKS)
        def _():
            send_chunk(t + AHEAD)

        @pl.when(t < CHUNKS)
        def _():
            drain(ybuf.at[t, pl.ds(0, NJ - 1)], y_recv.at[t])
            for copy in legs(t, True):
                copy.start()

        @pl.when(t == 1)
        def _():
            b_along_x()

        @pl.when(jnp.logical_and(t >= lag1, t < CHUNKS + lag1))
        def _():
            k = t - lag1
            first, second = legs(k, True), legs(k, False)
            for way in range(2):
                first[way].wait_recv()
                second[way].start()

        @pl.when(t == 2)
        def _():
            b_along_y()

        @pl.when(t == 3)
        def _():
            for copy in b_core():
                copy.start()

        @pl.when(t == lag2)
        def _():
            other = 1 - c
            for yy in range(NY):
                drain(bfull.at[yy, other], bc_recv.at[yy])

        @pl.when(t >= lag2)
        def _():
            k = t - lag2

            @pl.when(k % GROUP == 0)
            def _():
                own_half(k // GROUP)

            for copy in legs(k, False):
                copy.wait_recv()
            compute(k)

    drain(out_ref.at[pl.ds(0, (NJ - 1) * pairs)], c_recv)

    @pl.loop(0, CHUNKS)
    def _(k):
        drain(ybuf.at[k, pl.ds(0, NJ - 1)], y_send.at[k])
        for copy in legs(k, True) + legs(k, False):
            copy.wait_send()
        drain(cbuf.at[k, pl.ds(0, NJ - 1)], c_send.at[k])
        own_copy(k).wait()

    for i, d in enumerate((1, 2, 3, 4, -1, -2, -3)):
        zz = (z + d + NZ) % NZ

        @pl.when(zz // NZL == x // 2)
        def _():
            drain(bsend, bz_send.at[i])

    @pl.when(in_half)
    def _():
        for d in range(1, NX):
            drain(bfull.at[y, c, x % 2], bx_send.at[d - 1])

    for d in range(1, NY):
        drain(bfull.at[y, c], by_send.at[d - 1])
    for copy in b_core_copies():
        copy.wait_send()


def body(
    amplitudes, amplitude_map, integrals, integral_map, pair_list, occupied_energy, virtual_energy
):
    pair_count, rows, cols = amplitudes.shape
    q = pair_count // NJ // CHUNKS
    vmem = pl.BlockSpec(memory_space=pltpu.VMEM)
    hbm = pl.BlockSpec(memory_space=pl.ANY)
    smem = pl.BlockSpec(memory_space=pltpu.SMEM)
    dma = pltpu.SemaphoreType.DMA
    block = pltpu.VMEM((CHUNKS, NJ, q, rows, cols), jnp.bfloat16)
    return pl.pallas_call(
        kernel,
        out_shape=jax.ShapeDtypeStruct(amplitudes.shape, jnp.bfloat16),
        in_specs=[hbm, smem, hbm, smem, smem, smem, smem, vmem],
        out_specs=pl.BlockSpec(memory_space=pl.ANY),
        scratch_shapes=[
            pltpu.VMEM(amplitudes.shape, jnp.bfloat16),
            block,
            block,
            block,
            block,
            pltpu.VMEM((TILE, 256), jnp.bfloat16),
            pltpu.VMEM((NZL, TILE, 256), jnp.bfloat16),
            pltpu.VMEM((NY, NC, 2, 256, NZL * TILE), jnp.bfloat16),
            pltpu.VMEM((4, CHUNKS, q * rows, 256), jnp.float32),
            pltpu.VMEM((TILE, 128), jnp.float32),
            dma((CHUNKS,)),
            dma((CHUNKS,)),
            dma((CHUNKS, 2)),
            dma((CHUNKS, 2)),
            dma((CHUNKS, 2)),
            dma((CHUNKS, 2)),
            dma((CHUNKS,)),
            dma,
            dma((CHUNKS,)),
            dma((7,)),
            dma,
            dma((NX - 1,)),
            dma((2,)),
            dma((NY - 1,)),
            dma((NY,)),
            dma((NY,)),
            dma((NY,)),
            dma((2,)),
        ],
        compiler_params=pltpu.CompilerParams(
            collective_id=0, has_side_effects=True, vmem_limit_bytes=60 * 1024 * 1024
        ),
        cost_estimate=pl.CostEstimate(
            flops=2 * 1024 * 2048 * 1024, bytes_accessed=8 * 1024 * 1024, transcendentals=0
        ),
    )(
        amplitudes,
        amplitude_map,
        integrals,
        integral_map,
        pair_list.T,
        occupied_energy,
        virtual_energy,
        virtual_energy.reshape(1, -1),
    )


def solution(mesh):
    in_specs = (
        P(None, "blk", "grp"),
        P("blk", "grp"),
        P("blk", None),
        P("blk", None),
        P(),
        P(),
        P(),
    )
    out_specs = P(None, "blk", "grp")
    return jax.shard_map(body, mesh=mesh, in_specs=in_specs, out_specs=out_specs, check_vma=False)
```

```python
import jax
import jax.numpy as jnp
from jax import lax
from jax.experimental import pallas as pl
from jax.experimental.pallas import tpu as pltpu
from jax.sharding import PartitionSpec as P

MESH = pl.DeviceIdType.MESH
TILE = 64
NX, NZ, NZL, NJ, NY, NC = 4, 16, 8, 8, 4, 2
CHUNKS = 16
AHEAD = 3
GROUP = 4
HOPS, LAG = 8, 2


def drain(ref, sem):
    pltpu.make_async_copy(ref, ref, sem).wait()


def kernel(
    amp_ref,
    amp_map_ref,
    int_ref,
    int_map_ref,
    pair_ref,
    occ_ref,
    ve_smem,
    ve_row,
    out_ref,
    masked,
    zall,
    cbuf,
    bsend,
    bline,
    bfull,
    own_acc,
    erow,
    y_send,
    y_recv,
    z_send,
    z_recv,
    c_send,
    c_recv,
    own_sem,
    bz_send,
    bz_recv,
    bx_send,
    bx_recv,
    by_send,
    by_recv,
    bc_send,
    bc_recv,
    in_sem,
):
    b = lax.axis_index("blk")
    g = lax.axis_index("grp")
    x, zl = b // NZL, b % NZL
    h, j = g // NJ, g % NJ
    y, c = j // NC, j % NC
    z = h * NZL + zl
    pairs = amp_ref.shape[0] // NJ
    q = pairs // CHUNKS
    half_cols = NJ * 128

    def at_z(zz):
        zz = (zz + NZ) % NZ
        return (x * NZL + zz % NZL, (zz // NZL) * NJ + j)

    def at_j(jj):
        return (b, h * NJ + jj)

    def at_x(xx):
        return (xx * NZL + zl, g)

    ybuf, zbuf = zall.at[0], zall.at[HOPS]

    peers = [at_z(z + d) for d in (1, 2, 3, 4, -1, -2, -3, -4)]
    peers += [at_j((j + d) % NJ) for d in range(1, NJ)]
    peers += [at_x((x + d) % NX) for d in range(1, NX)]
    barrier = pltpu.get_barrier_semaphore()
    for peer in peers:
        pl.semaphore_signal(barrier, inc=1, device_id=peer, device_id_type=MESH)

    loads = [
        pltpu.make_async_copy(amp_ref, masked, in_sem.at[0]),
        pltpu.make_async_copy(
            int_ref.at[:, pl.ds(pl.multiple_of(j * 256, 128), 256)], bsend, in_sem.at[1]
        ),
    ]
    for load in loads:
        load.start()

    @pl.loop(0, TILE)
    def _(r):
        erow[pl.ds(r, 1), :] = jnp.full((1, 128), ve_smem[b * TILE + r], jnp.float32)

    lane = lax.broadcasted_iota(jnp.int32, (1, 128), 1)
    keep0 = amp_map_ref[0, 0].astype(jnp.float32)
    keep1 = amp_map_ref[0, 1].astype(jnp.float32)
    amp_mask = jnp.where(lane < TILE, keep0, keep1).astype(jnp.bfloat16)

    loads[0].wait()

    @pl.loop(0, NJ * pairs)
    def _(p):
        masked[p] = masked[p] * amp_mask

    ybuf[:, j] = masked[pl.ds(j * pairs, pairs)].reshape(CHUNKS, q, TILE, 128)
    loads[1].wait()
    for half in range(2):
        tile = 4 * j + 2 * half
        keep0 = int_map_ref[0, tile].astype(jnp.float32)
        keep1 = int_map_ref[0, tile + 1].astype(jnp.float32)
        int_mask = jnp.where(lane < TILE, keep0, keep1).astype(jnp.bfloat16)
        cols = slice(half * 128, half * 128 + 128)
        bsend[:, cols] = bsend[:, cols] * int_mask

    pl.semaphore_wait(barrier, len(peers))

    def send_chunk(k):
        for d in range(1, NJ):
            jj = (j + d) % NJ
            pltpu.make_async_remote_copy(
                src_ref=masked.at[pl.ds(jj * pairs + k * q, q)],
                dst_ref=ybuf.at[k, j],
                send_sem=y_send.at[k],
                recv_sem=y_recv.at[k],
                device_id=at_j(jj),
                device_id_type=MESH,
            ).start()

    send_chunk(0)

    in_half = x // 2 == h
    for i, d in enumerate((1, 2, 3, 4, -1, -2, -3)):
        zz = (z + d + NZ) % NZ

        @pl.when(zz // NZL == x // 2)
        def _():
            pltpu.make_async_remote_copy(
                src_ref=bsend,
                dst_ref=bline.at[zl],
                send_sem=bz_send.at[i],
                recv_sem=bz_recv,
                device_id=at_z(zz),
                device_id_type=MESH,
            ).start()

    for k in range(1, AHEAD):
        send_chunk(k)
    bline[zl] = bsend[...]

    def hop(m, k, way):
        return pltpu.make_async_remote_copy(
            src_ref=zall.at[m - 1, k, pl.ds(4 * way, 4)],
            dst_ref=zall.at[m, k, pl.ds(4 * way, 4)],
            send_sem=z_send.at[m - 1, k, way],
            recv_sem=z_recv.at[m - 1, k, way],
            device_id=at_z(z + (1 if way == 0 else -1)),
            device_id_type=MESH,
        )

    def b_along_x():
        @pl.when(in_half)
        def _():
            drain(bline.at[pl.ds(0, NZL - 1)], bz_recv)
            bfull[y, c, x % 2] = bline[...].reshape(NZL * TILE, 256).T
            for d in range(1, NX):
                pltpu.make_async_remote_copy(
                    src_ref=bfull.at[y, c, x % 2],
                    dst_ref=bfull.at[y, c, x % 2],
                    send_sem=bx_send.at[d - 1],
                    recv_sem=bx_recv.at[x % 2],
                    device_id=at_x((x + d) % NX),
                    device_id_type=MESH,
                ).start()

    def b_along_y():
        for xx in range(2):

            @pl.when(x != 2 * h + xx)
            def _():
                drain(bfull.at[y, c, xx], bx_recv.at[xx])

        for d in range(1, NY):
            pltpu.make_async_remote_copy(
                src_ref=bfull.at[y, c],
                dst_ref=bfull.at[y, c],
                send_sem=by_send.at[d - 1],
                recv_sem=by_recv.at[y],
                device_id=at_j(((y + d) % NY) * NC + c),
                device_id_type=MESH,
            ).start()

    def b_core():
        for d in range(1, NY):
            yy = (y + d) % NY
            drain(bfull.at[yy, c], by_recv.at[yy])
        return b_core_copies()

    def b_core_copies():
        return [
            pltpu.make_async_remote_copy(
                src_ref=bfull.at[yy, c],
                dst_ref=bfull.at[yy, c],
                send_sem=bc_send.at[yy],
                recv_sem=bc_recv.at[yy],
                device_id=at_j(y * NC + 1 - c),
                device_id_type=MESH,
            )
            for yy in range(NY)
        ]

    def weights(hh, i, n):
        cols = pl.ds(pl.multiple_of((n % 2) * 256, 256), 256)
        return bfull[2 * hh + i // 2, i % 2, n // 2, :, cols]

    def rows_of(buf, first, count, i):
        blocks = [
            buf[pl.ds(first, count), 2 * i + e].reshape(count * q * TILE, 128) for e in range(2)
        ]
        return jnp.concatenate(blocks, axis=1)

    def own_half(group):
        @pl.loop(0, 4)
        def _(n):
            acc = jnp.zeros((GROUP * q * TILE, 256), jnp.float32)
            for i in range(4):
                acc += jnp.dot(
                    rows_of(ybuf, group * GROUP, GROUP, i),
                    weights(h, i, n),
                    preferred_element_type=jnp.float32,
                )
            own_acc[n, pl.ds(group * GROUP, GROUP)] = acc.reshape(GROUP, q * TILE, 256)

    def compute(k):
        @pl.loop(0, 4)
        def _(n):
            acc = own_acc[n, k]
            for i in range(4):
                acc += jnp.dot(
                    rows_of(zbuf, k, 1, i),
                    weights(1 - h, i, n),
                    preferred_element_type=jnp.float32,
                )
            ladder = acc.astype(jnp.bfloat16).astype(jnp.float32)
            for e in range(2):
                start = pl.multiple_of(h * half_cols + n * 256 + e * 128, 128)
                virt = erow[...] + ve_row[:, pl.ds(start, 128)]
                for p in range(q):
                    pair = j * pairs + k * q + p
                    shift = occ_ref[pair_ref[0, pair]] + occ_ref[pair_ref[1, pair]]
                    block = ladder[p * TILE : (p + 1) * TILE, e * 128 : (e + 1) * 128]
                    cbuf[k, 2 * n + e, p] = (block / (virt - shift)).astype(jnp.bfloat16)

        for d in range(1, NJ):
            jj = (j + d) % NJ
            pltpu.make_async_remote_copy(
                src_ref=cbuf.at[k, jj],
                dst_ref=out_ref.at[pl.ds(j * pairs + k * q, q)],
                send_sem=c_send.at[k],
                recv_sem=c_recv,
                device_id=at_j(jj),
                device_id_type=MESH,
            ).start()
        own_copy(k).start()

    def own_copy(k):
        return pltpu.make_async_copy(
            cbuf.at[k, j], out_ref.at[pl.ds(j * pairs + k * q, q)], own_sem.at[k]
        )

    @pl.loop(0, CHUNKS + LAG * HOPS)
    def _(s):
        @pl.when(s + AHEAD < CHUNKS)
        def _():
            send_chunk(s + AHEAD)

        for m in range(HOPS, 0, -1):
            k = s - LAG * (m - 1)

            @pl.when(jnp.logical_and(k >= 0, k < CHUNKS))
            def _():
                if m == 1:
                    drain(ybuf.at[k, pl.ds(0, NJ - 1)], y_recv.at[k])
                for way in range(2):
                    if m > 1:
                        hop(m - 1, k, way).wait_recv()
                    hop(m, k, way).start()

        @pl.when(s == 4)
        def _():
            b_along_x()

        @pl.when(s == 6)
        def _():
            b_along_y()

        @pl.when(s == 9)
        def _():
            for copy in b_core():
                copy.start()

        @pl.when(s == 11)
        def _():
            for yy in range(NY):
                drain(bfull.at[yy, 1 - c], bc_recv.at[yy])

        @pl.when(jnp.logical_and(s >= 12, s < 12 + CHUNKS // GROUP))
        def _():
            own_half(s - 12)

        @pl.when(s >= LAG * HOPS)
        def _():
            k = s - LAG * HOPS
            for way in range(2):
                hop(HOPS, k, way).wait_recv()
            compute(k)

    drain(out_ref.at[pl.ds(0, (NJ - 1) * pairs)], c_recv)

    @pl.loop(0, CHUNKS)
    def _(k):
        drain(ybuf.at[k, pl.ds(0, NJ - 1)], y_send.at[k])
        for m in range(1, HOPS + 1):
            for way in range(2):
                hop(m, k, way).wait_send()
        drain(cbuf.at[k, pl.ds(0, NJ - 1)], c_send.at[k])
        own_copy(k).wait()

    for i, d in enumerate((1, 2, 3, 4, -1, -2, -3)):
        zz = (z + d + NZ) % NZ

        @pl.when(zz // NZL == x // 2)
        def _():
            drain(bsend, bz_send.at[i])

    @pl.when(in_half)
    def _():
        for d in range(1, NX):
            drain(bfull.at[y, c, x % 2], bx_send.at[d - 1])

    for d in range(1, NY):
        drain(bfull.at[y, c], by_send.at[d - 1])
    for copy in b_core_copies():
        copy.wait_send()


def body(
    amplitudes, amplitude_map, integrals, integral_map, pair_list, occupied_energy, virtual_energy
):
    pair_count, rows, cols = amplitudes.shape
    q = pair_count // NJ // CHUNKS
    vmem = pl.BlockSpec(memory_space=pltpu.VMEM)
    hbm = pl.BlockSpec(memory_space=pl.ANY)
    smem = pl.BlockSpec(memory_space=pltpu.SMEM)
    dma = pltpu.SemaphoreType.DMA
    block = (CHUNKS, NJ, q, rows, cols)
    return pl.pallas_call(
        kernel,
        out_shape=jax.ShapeDtypeStruct(amplitudes.shape, jnp.bfloat16),
        in_specs=[hbm, smem, hbm, smem, smem, smem, smem, vmem],
        out_specs=pl.BlockSpec(memory_space=pl.ANY),
        scratch_shapes=[
            pltpu.VMEM(amplitudes.shape, jnp.bfloat16),
            pltpu.VMEM((HOPS + 1, *block), jnp.bfloat16),
            pltpu.VMEM(block, jnp.bfloat16),
            pltpu.VMEM((TILE, 256), jnp.bfloat16),
            pltpu.VMEM((NZL, TILE, 256), jnp.bfloat16),
            pltpu.VMEM((NY, NC, 2, 256, NZL * TILE), jnp.bfloat16),
            pltpu.VMEM((4, CHUNKS, q * rows, 256), jnp.float32),
            pltpu.VMEM((TILE, 128), jnp.float32),
            dma((CHUNKS,)),
            dma((CHUNKS,)),
            dma((HOPS, CHUNKS, 2)),
            dma((HOPS, CHUNKS, 2)),
            dma((CHUNKS,)),
            dma,
            dma((CHUNKS,)),
            dma((7,)),
            dma,
            dma((NX - 1,)),
            dma((2,)),
            dma((NY - 1,)),
            dma((NY,)),
            dma((NY,)),
            dma((NY,)),
            dma((2,)),
        ],
        compiler_params=pltpu.CompilerParams(
            collective_id=0, has_side_effects=True, vmem_limit_bytes=60 * 1024 * 1024
        ),
        cost_estimate=pl.CostEstimate(
            flops=2 * 1024 * 2048 * 1024, bytes_accessed=8 * 1024 * 1024, transcendentals=0
        ),
    )(
        amplitudes,
        amplitude_map,
        integrals,
        integral_map,
        pair_list.T,
        occupied_energy,
        virtual_energy,
        virtual_energy.reshape(1, -1),
    )


def solution(mesh):
    in_specs = (
        P(None, "blk", "grp"),
        P("blk", "grp"),
        P("blk", None),
        P("blk", None),
        P(),
        P(),
        P(),
    )
    out_specs = P(None, "blk", "grp")
    return jax.shard_map(body, mesh=mesh, in_specs=in_specs, out_specs=out_specs, check_vma=False)
```

```python
import jax
import jax.numpy as jnp
from jax import lax
from jax.experimental import pallas as pl
from jax.experimental.pallas import tpu as pltpu
from jax.sharding import PartitionSpec as P

MESH = pl.DeviceIdType.MESH
TILE = 64
NX, NZ, NZL, NJ, NY, NC = 4, 16, 8, 8, 4, 2
CHUNKS = 8
AHEAD = 3
GROUP = 2
LEGS = (5, 3)


def drain(ref, sem):
    pltpu.make_async_copy(ref, ref, sem).wait()


def kernel(
    amp_ref,
    amp_map_ref,
    int_ref,
    int_map_ref,
    pair_ref,
    occ_ref,
    ve_smem,
    ve_row,
    out_ref,
    masked,
    ybuf,
    relay,
    zbuf,
    cbuf,
    bline,
    bfull,
    own_acc,
    erow,
    y_send,
    y_recv,
    z_send,
    z_recv,
    f_send,
    f_recv,
    c_send,
    c_recv,
    own_sem,
    bz_send,
    bz_recv,
    bx_send,
    bx_recv,
    by_send,
    by_recv,
    bc_send,
    bc_recv,
    in_sem,
):
    b = lax.axis_index("blk")
    g = lax.axis_index("grp")
    x, zl = b // NZL, b % NZL
    h, j = g // NJ, g % NJ
    y, c = j // NC, j % NC
    z = h * NZL + zl
    pairs = amp_ref.shape[0] // NJ
    q = pairs // CHUNKS
    half_cols = NJ * 128

    def at_z(zz):
        zz = (zz + NZ) % NZ
        return (x * NZL + zz % NZL, (zz // NZL) * NJ + j)

    def at_j(jj):
        return (b, h * NJ + jj)

    def at_x(xx):
        return (xx * NZL + zl, g)

    peers = [at_z(z + d) for d in (1, -1, 3, -3, 5, -5)]
    peers += [at_j((j + d) % NJ) for d in range(1, NJ)]
    peers += [at_x((x + d) % NX) for d in range(1, NX)]
    barrier = pltpu.get_barrier_semaphore()
    for peer in peers:
        pl.semaphore_signal(barrier, inc=1, device_id=peer, device_id_type=MESH)

    loads = [
        pltpu.make_async_copy(amp_ref, masked, in_sem.at[0]),
        pltpu.make_async_copy(
            int_ref.at[:, pl.ds(pl.multiple_of(j * 256, 128), 256)], bline.at[zl], in_sem.at[1]
        ),
    ]
    for load in loads:
        load.start()

    @pl.loop(0, TILE)
    def _(r):
        erow[pl.ds(r, 1), :] = jnp.full((1, 128), ve_smem[b * TILE + r], jnp.float32)

    lane = lax.broadcasted_iota(jnp.int32, (1, 128), 1)
    keep0 = amp_map_ref[0, 0].astype(jnp.float32)
    keep1 = amp_map_ref[0, 1].astype(jnp.float32)
    amp_mask = jnp.where(lane < TILE, keep0, keep1).astype(jnp.bfloat16)

    loads[0].wait()

    @pl.loop(0, NJ * pairs)
    def _(p):
        masked[p] = masked[p] * amp_mask

    ybuf[:, j] = masked[pl.ds(j * pairs, pairs)].reshape(CHUNKS, q, TILE, 128)
    loads[1].wait()
    for half in range(2):
        tile = 4 * j + 2 * half
        keep0 = int_map_ref[0, tile].astype(jnp.float32)
        keep1 = int_map_ref[0, tile + 1].astype(jnp.float32)
        int_mask = jnp.where(lane < TILE, keep0, keep1).astype(jnp.bfloat16)
        cols = slice(half * 128, half * 128 + 128)
        bline[zl, :, cols] = bline[zl, :, cols] * int_mask

    pl.semaphore_wait(barrier, len(peers))

    def send_chunk(k):
        for d in range(1, NJ):
            jj = (j + d) % NJ
            pltpu.make_async_remote_copy(
                src_ref=masked.at[pl.ds(jj * pairs + k * q, q)],
                dst_ref=ybuf.at[k, j],
                send_sem=y_send.at[k],
                recv_sem=y_recv.at[k],
                device_id=at_j(jj),
                device_id_type=MESH,
            ).start()

    send_chunk(0)

    def b_hop(r, way):
        step = 1 if way == 0 else -1
        slot = (z - step * (r - 1) + NZ) % NZL
        return pltpu.make_async_remote_copy(
            src_ref=bline.at[slot],
            dst_ref=bline.at[slot],
            send_sem=bz_send.at[4 * way + r - 1],
            recv_sem=bz_recv.at[4 * way + r - 1],
            device_id=at_z(z + step),
            device_id_type=MESH,
        )

    def b_arrived(r, way):
        step = 1 if way == 0 else -1
        drain(bline.at[(z - step * r + NZ) % NZL], bz_recv.at[4 * way + r - 1])

    for way in range(2):
        b_hop(1, way).start()
    for k in range(1, AHEAD):
        send_chunk(k)
        for way in range(2):
            b_arrived(k, way)
            b_hop(k + 1, way).start()

    def legs(k, first):
        src, dst = (ybuf, relay) if first else (relay, zbuf)
        hops = LEGS[0] if first else LEGS[1]
        ssem, rsem = (z_send, z_recv) if first else (f_send, f_recv)
        return [
            pltpu.make_async_remote_copy(
                src_ref=src.at[k, pl.ds(4 * way, 4)],
                dst_ref=dst.at[k, pl.ds(4 * way, 4)],
                send_sem=ssem.at[k, way],
                recv_sem=rsem.at[k, way],
                device_id=at_z(z + (hops if way == 0 else -hops)),
                device_id_type=MESH,
            )
            for way in range(2)
        ]

    in_half = x // 2 == h

    def b_along_x():
        b_arrived(4, 0)

        @pl.when(in_half)
        def _():
            bfull[y, c, x % 2] = bline[...].reshape(NZL * TILE, 256).T
            for d in range(1, NX):
                pltpu.make_async_remote_copy(
                    src_ref=bfull.at[y, c, x % 2],
                    dst_ref=bfull.at[y, c, x % 2],
                    send_sem=bx_send.at[d - 1],
                    recv_sem=bx_recv.at[x % 2],
                    device_id=at_x((x + d) % NX),
                    device_id_type=MESH,
                ).start()

    def b_along_y():
        for xx in range(2):

            @pl.when(x != 2 * h + xx)
            def _():
                drain(bfull.at[y, c, xx], bx_recv.at[xx])

        for d in range(1, NY):
            pltpu.make_async_remote_copy(
                src_ref=bfull.at[y, c],
                dst_ref=bfull.at[y, c],
                send_sem=by_send.at[d - 1],
                recv_sem=by_recv.at[y],
                device_id=at_j(((y + d) % NY) * NC + c),
                device_id_type=MESH,
            ).start()

    def b_core():
        for d in range(1, NY):
            yy = (y + d) % NY
            drain(bfull.at[yy, c], by_recv.at[yy])
        return b_core_copies()

    def b_core_copies():
        return [
            pltpu.make_async_remote_copy(
                src_ref=bfull.at[yy, c],
                dst_ref=bfull.at[yy, c],
                send_sem=bc_send.at[yy],
                recv_sem=bc_recv.at[yy],
                device_id=at_j(y * NC + 1 - c),
                device_id_type=MESH,
            )
            for yy in range(NY)
        ]

    def weights(hh, i, n):
        cols = pl.ds(pl.multiple_of((n % 2) * 256, 256), 256)
        return bfull[2 * hh + i // 2, i % 2, n // 2, :, cols]

    def rows_of(buf, first, count, i):
        blocks = [
            buf[pl.ds(first, count), 2 * i + e].reshape(count * q * TILE, 128) for e in range(2)
        ]
        return jnp.concatenate(blocks, axis=1)

    def own_half(group):
        @pl.loop(0, 4)
        def _(n):
            acc = jnp.zeros((GROUP * q * TILE, 256), jnp.float32)
            for i in range(4):
                acc += jnp.dot(
                    rows_of(ybuf, group * GROUP, GROUP, i),
                    weights(h, i, n),
                    preferred_element_type=jnp.float32,
                )
            own_acc[n, pl.ds(group * GROUP, GROUP)] = acc.reshape(GROUP, q * TILE, 256)

    def compute(k):
        @pl.loop(0, 4)
        def _(n):
            acc = own_acc[n, k]
            for i in range(4):
                acc += jnp.dot(
                    rows_of(zbuf, k, 1, i),
                    weights(1 - h, i, n),
                    preferred_element_type=jnp.float32,
                )
            ladder = acc.astype(jnp.bfloat16).astype(jnp.float32)
            for e in range(2):
                start = pl.multiple_of(h * half_cols + n * 256 + e * 128, 128)
                virt = erow[...] + ve_row[:, pl.ds(start, 128)]
                for p in range(q):
                    pair = j * pairs + k * q + p
                    shift = occ_ref[pair_ref[0, pair]] + occ_ref[pair_ref[1, pair]]
                    block = ladder[p * TILE : (p + 1) * TILE, e * 128 : (e + 1) * 128]
                    cbuf[k, 2 * n + e, p] = (block / (virt - shift)).astype(jnp.bfloat16)

        for d in range(1, NJ):
            jj = (j + d) % NJ
            pltpu.make_async_remote_copy(
                src_ref=cbuf.at[k, jj],
                dst_ref=out_ref.at[pl.ds(j * pairs + k * q, q)],
                send_sem=c_send.at[k],
                recv_sem=c_recv,
                device_id=at_j(jj),
                device_id_type=MESH,
            ).start()
        own_copy(k).start()

    def own_copy(k):
        return pltpu.make_async_copy(
            cbuf.at[k, j], out_ref.at[pl.ds(j * pairs + k * q, q)], own_sem.at[k]
        )

    lag1, lag2 = 2, 4

    @pl.loop(0, CHUNKS + lag2)
    def _(t):
        @pl.when(t + AHEAD < CHUNKS)
        def _():
            send_chunk(t + AHEAD)

        @pl.when(t < CHUNKS)
        def _():
            drain(ybuf.at[t, pl.ds(0, NJ - 1)], y_recv.at[t])
            for copy in legs(t, True):
                copy.start()

        @pl.when(t == 0)
        def _():
            b_arrived(3, 0)
            b_arrived(3, 1)
            b_hop(4, 0).start()

        @pl.when(t == 1)
        def _():
            b_along_x()

        @pl.when(jnp.logical_and(t >= lag1, t < CHUNKS + lag1))
        def _():
            k = t - lag1
            first, second = legs(k, True), legs(k, False)
            for way in range(2):
                first[way].wait_recv()
                second[way].start()

        @pl.when(t == 2)
        def _():
            b_along_y()

        @pl.when(t == 3)
        def _():
            for copy in b_core():
                copy.start()

        @pl.when(t == lag2)
        def _():
            other = 1 - c
            for yy in range(NY):
                drain(bfull.at[yy, other], bc_recv.at[yy])

        @pl.when(t >= lag2)
        def _():
            k = t - lag2

            @pl.when(k % GROUP == 0)
            def _():
                own_half(k // GROUP)

            for copy in legs(k, False):
                copy.wait_recv()
            compute(k)

    drain(out_ref.at[pl.ds(0, (NJ - 1) * pairs)], c_recv)

    @pl.loop(0, CHUNKS)
    def _(k):
        drain(ybuf.at[k, pl.ds(0, NJ - 1)], y_send.at[k])
        for copy in legs(k, True) + legs(k, False):
            copy.wait_send()
        drain(cbuf.at[k, pl.ds(0, NJ - 1)], c_send.at[k])
        own_copy(k).wait()

    for way in range(2):
        for r in range(1, 5 - way):
            b_hop(r, way).wait_send()

    @pl.when(in_half)
    def _():
        for d in range(1, NX):
            drain(bfull.at[y, c, x % 2], bx_send.at[d - 1])

    for d in range(1, NY):
        drain(bfull.at[y, c], by_send.at[d - 1])
    for copy in b_core_copies():
        copy.wait_send()


def body(
    amplitudes, amplitude_map, integrals, integral_map, pair_list, occupied_energy, virtual_energy
):
    pair_count, rows, cols = amplitudes.shape
    q = pair_count // NJ // CHUNKS
    vmem = pl.BlockSpec(memory_space=pltpu.VMEM)
    hbm = pl.BlockSpec(memory_space=pl.ANY)
    smem = pl.BlockSpec(memory_space=pltpu.SMEM)
    dma = pltpu.SemaphoreType.DMA
    block = pltpu.VMEM((CHUNKS, NJ, q, rows, cols), jnp.bfloat16)
    return pl.pallas_call(
        kernel,
        out_shape=jax.ShapeDtypeStruct(amplitudes.shape, jnp.bfloat16),
        in_specs=[hbm, smem, hbm, smem, smem, smem, smem, vmem],
        out_specs=pl.BlockSpec(memory_space=pl.ANY),
        scratch_shapes=[
            pltpu.VMEM(amplitudes.shape, jnp.bfloat16),
            block,
            block,
            block,
            block,
            pltpu.VMEM((NZL, TILE, 256), jnp.bfloat16),
            pltpu.VMEM((NY, NC, 2, 256, NZL * TILE), jnp.bfloat16),
            pltpu.VMEM((4, CHUNKS, q * rows, 256), jnp.float32),
            pltpu.VMEM((TILE, 128), jnp.float32),
            dma((CHUNKS,)),
            dma((CHUNKS,)),
            dma((CHUNKS, 2)),
            dma((CHUNKS, 2)),
            dma((CHUNKS, 2)),
            dma((CHUNKS, 2)),
            dma((CHUNKS,)),
            dma,
            dma((CHUNKS,)),
            dma((7,)),
            dma((7,)),
            dma((NX - 1,)),
            dma((2,)),
            dma((NY - 1,)),
            dma((NY,)),
            dma((NY,)),
            dma((NY,)),
            dma((2,)),
        ],
        compiler_params=pltpu.CompilerParams(
            collective_id=0, has_side_effects=True, vmem_limit_bytes=60 * 1024 * 1024
        ),
        cost_estimate=pl.CostEstimate(
            flops=2 * 1024 * 2048 * 1024, bytes_accessed=8 * 1024 * 1024, transcendentals=0
        ),
    )(
        amplitudes,
        amplitude_map,
        integrals,
        integral_map,
        pair_list.T,
        occupied_energy,
        virtual_energy,
        virtual_energy.reshape(1, -1),
    )


def solution(mesh):
    in_specs = (
        P(None, "blk", "grp"),
        P("blk", "grp"),
        P("blk", None),
        P("blk", None),
        P(),
        P(),
        P(),
    )
    out_specs = P(None, "blk", "grp")
    return jax.shard_map(body, mesh=mesh, in_specs=in_specs, out_specs=out_specs, check_vma=False)
```

```python
import jax
import jax.numpy as jnp
from jax import lax
from jax.experimental import pallas as pl
from jax.experimental.pallas import tpu as pltpu
from jax.sharding import PartitionSpec as P

MESH = pl.DeviceIdType.MESH
TILE = 64
NX, NZ, NZL, NJ, NY, NC = 4, 16, 8, 8, 4, 2
CHUNKS = 16
AHEAD = 4
GROUP = 4
LEGS = (5, 3)


def drain(ref, sem):
    pltpu.make_async_copy(ref, ref, sem).wait()


def kernel(
    amp_ref,
    amp_map_ref,
    int_ref,
    int_map_ref,
    pair_ref,
    occ_ref,
    ve_smem,
    ve_row,
    out_ref,
    masked,
    ybuf,
    relay,
    zbuf,
    cbuf,
    bline,
    bfull,
    own_acc,
    erow,
    y_send,
    y_recv,
    z_send,
    z_recv,
    f_send,
    f_recv,
    c_send,
    c_recv,
    own_sem,
    bz_send,
    bz_recv,
    bx_send,
    bx_recv,
    by_send,
    by_recv,
    bc_send,
    bc_recv,
    in_sem,
):
    b = lax.axis_index("blk")
    g = lax.axis_index("grp")
    x, zl = b // NZL, b % NZL
    h, j = g // NJ, g % NJ
    y, c = j // NC, j % NC
    z = h * NZL + zl
    pairs = amp_ref.shape[0] // NJ
    q = pairs // CHUNKS
    half_cols = NJ * 128

    def at_z(zz):
        zz = (zz + NZ) % NZ
        return (x * NZL + zz % NZL, (zz // NZL) * NJ + j)

    def at_j(jj):
        return (b, h * NJ + jj)

    def at_x(xx):
        return (xx * NZL + zl, g)

    peers = [at_z(z + d) for d in (1, -1, 3, -3, 5, -5)]
    peers += [at_j((j + d) % NJ) for d in range(1, NJ)]
    peers += [at_x((x + d) % NX) for d in range(1, NX)]
    barrier = pltpu.get_barrier_semaphore()
    for peer in peers:
        pl.semaphore_signal(barrier, inc=1, device_id=peer, device_id_type=MESH)

    loads = [
        pltpu.make_async_copy(amp_ref, masked, in_sem.at[0]),
        pltpu.make_async_copy(
            int_ref.at[:, pl.ds(pl.multiple_of(j * 256, 128), 256)], bline.at[zl], in_sem.at[1]
        ),
    ]
    for load in loads:
        load.start()

    @pl.loop(0, TILE)
    def _(r):
        erow[pl.ds(r, 1), :] = jnp.full((1, 128), ve_smem[b * TILE + r], jnp.float32)

    lane = lax.broadcasted_iota(jnp.int32, (1, 128), 1)
    keep0 = amp_map_ref[0, 0].astype(jnp.float32)
    keep1 = amp_map_ref[0, 1].astype(jnp.float32)
    amp_mask = jnp.where(lane < TILE, keep0, keep1).astype(jnp.bfloat16)

    loads[0].wait()

    @pl.loop(0, NJ * pairs)
    def _(p):
        masked[p] = masked[p] * amp_mask

    ybuf[:, j] = masked[pl.ds(j * pairs, pairs)].reshape(CHUNKS, q, TILE, 128)
    loads[1].wait()
    for half in range(2):
        tile = 4 * j + 2 * half
        keep0 = int_map_ref[0, tile].astype(jnp.float32)
        keep1 = int_map_ref[0, tile + 1].astype(jnp.float32)
        int_mask = jnp.where(lane < TILE, keep0, keep1).astype(jnp.bfloat16)
        cols = slice(half * 128, half * 128 + 128)
        bline[zl, :, cols] = bline[zl, :, cols] * int_mask

    pl.semaphore_wait(barrier, len(peers))

    def send_chunk(k):
        for d in range(1, NJ):
            jj = (j + d) % NJ
            pltpu.make_async_remote_copy(
                src_ref=masked.at[pl.ds(jj * pairs + k * q, q)],
                dst_ref=ybuf.at[k, j],
                send_sem=y_send.at[k],
                recv_sem=y_recv.at[k],
                device_id=at_j(jj),
                device_id_type=MESH,
            ).start()

    send_chunk(0)

    def b_hop(r, way):
        step = 1 if way == 0 else -1
        slot = (z - step * (r - 1) + NZ) % NZL
        return pltpu.make_async_remote_copy(
            src_ref=bline.at[slot],
            dst_ref=bline.at[slot],
            send_sem=bz_send.at[4 * way + r - 1],
            recv_sem=bz_recv.at[4 * way + r - 1],
            device_id=at_z(z + step),
            device_id_type=MESH,
        )

    def b_arrived(r, way):
        step = 1 if way == 0 else -1
        drain(bline.at[(z - step * r + NZ) % NZL], bz_recv.at[4 * way + r - 1])

    for way in range(2):
        b_hop(1, way).start()
    for k in range(1, AHEAD):
        send_chunk(k)

    def legs(k, first):
        src, dst = (ybuf, relay) if first else (relay, zbuf)
        hops = LEGS[0] if first else LEGS[1]
        ssem, rsem = (z_send, z_recv) if first else (f_send, f_recv)
        return [
            pltpu.make_async_remote_copy(
                src_ref=src.at[k, pl.ds(4 * way, 4)],
                dst_ref=dst.at[k, pl.ds(4 * way, 4)],
                send_sem=ssem.at[k, way],
                recv_sem=rsem.at[k, way],
                device_id=at_z(z + (hops if way == 0 else -hops)),
                device_id_type=MESH,
            )
            for way in range(2)
        ]

    in_half = x // 2 == h

    def b_along_x():
        b_arrived(4, 0)

        @pl.when(in_half)
        def _():
            bfull[y, c, x % 2] = bline[...].reshape(NZL * TILE, 256).T
            for d in range(1, NX):
                pltpu.make_async_remote_copy(
                    src_ref=bfull.at[y, c, x % 2],
                    dst_ref=bfull.at[y, c, x % 2],
                    send_sem=bx_send.at[d - 1],
                    recv_sem=bx_recv.at[x % 2],
                    device_id=at_x((x + d) % NX),
                    device_id_type=MESH,
                ).start()

    def b_along_y():
        for xx in range(2):

            @pl.when(x != 2 * h + xx)
            def _():
                drain(bfull.at[y, c, xx], bx_recv.at[xx])

        for d in range(1, NY):
            pltpu.make_async_remote_copy(
                src_ref=bfull.at[y, c],
                dst_ref=bfull.at[y, c],
                send_sem=by_send.at[d - 1],
                recv_sem=by_recv.at[y],
                device_id=at_j(((y + d) % NY) * NC + c),
                device_id_type=MESH,
            ).start()

    def b_core():
        for d in range(1, NY):
            yy = (y + d) % NY
            drain(bfull.at[yy, c], by_recv.at[yy])
        return b_core_copies()

    def b_core_copies():
        return [
            pltpu.make_async_remote_copy(
                src_ref=bfull.at[yy, c],
                dst_ref=bfull.at[yy, c],
                send_sem=bc_send.at[yy],
                recv_sem=bc_recv.at[yy],
                device_id=at_j(y * NC + 1 - c),
                device_id_type=MESH,
            )
            for yy in range(NY)
        ]

    def weights(hh, i, n):
        cols = pl.ds(pl.multiple_of((n % 2) * 256, 256), 256)
        return bfull[2 * hh + i // 2, i % 2, n // 2, :, cols]

    def rows_of(buf, first, count, i):
        blocks = [
            buf[pl.ds(first, count), 2 * i + e].reshape(count * q * TILE, 128) for e in range(2)
        ]
        return jnp.concatenate(blocks, axis=1)

    def own_half(group):
        @pl.loop(0, 4)
        def _(n):
            acc = jnp.zeros((GROUP * q * TILE, 256), jnp.float32)
            for i in range(4):
                acc += jnp.dot(
                    rows_of(ybuf, group * GROUP, GROUP, i),
                    weights(h, i, n),
                    preferred_element_type=jnp.float32,
                )
            own_acc[n, pl.ds(group * GROUP, GROUP)] = acc.reshape(GROUP, q * TILE, 256)

    def compute(k):
        @pl.loop(0, 4)
        def _(step):
            n = (step + y) % 4
            acc = own_acc[n, k]
            for i in range(4):
                acc += jnp.dot(
                    rows_of(zbuf, k, 1, i),
                    weights(1 - h, i, n),
                    preferred_element_type=jnp.float32,
                )
            ladder = acc.astype(jnp.bfloat16).astype(jnp.float32)
            for e in range(2):
                start = pl.multiple_of(h * half_cols + n * 256 + e * 128, 128)
                virt = erow[...] + ve_row[:, pl.ds(start, 128)]
                for p in range(q):
                    pair = j * pairs + k * q + p
                    shift = occ_ref[pair_ref[0, pair]] + occ_ref[pair_ref[1, pair]]
                    block = ladder[p * TILE : (p + 1) * TILE, e * 128 : (e + 1) * 128]
                    cbuf[k, 2 * n + e, p] = (block / (virt - shift)).astype(jnp.bfloat16)

            for e in range(2):
                jj = 2 * n + e

                @pl.when(jj != j)
                def _():
                    pltpu.make_async_remote_copy(
                        src_ref=cbuf.at[k, jj],
                        dst_ref=out_ref.at[pl.ds(j * pairs + k * q, q)],
                        send_sem=c_send.at[k],
                        recv_sem=c_recv,
                        device_id=at_j(jj),
                        device_id_type=MESH,
                    ).start()

        own_copy(k).start()

    def own_copy(k):
        return pltpu.make_async_copy(
            cbuf.at[k, j], out_ref.at[pl.ds(j * pairs + k * q, q)], own_sem.at[k]
        )

    lag1, lag2 = 8, 16

    @pl.loop(0, CHUNKS + lag2)
    def _(t):
        @pl.when(t + AHEAD < CHUNKS)
        def _():
            send_chunk(t + AHEAD)

        @pl.when(t < CHUNKS)
        def _():
            drain(ybuf.at[t, pl.ds(0, NJ - 1)], y_recv.at[t])
            for copy in legs(t, True):
                copy.start()

        for r in range(1, 4):

            @pl.when(t == r - 1)
            def _():
                for way in range(2):
                    b_arrived(r, way)
                    if r + way < 4:
                        b_hop(r + 1, way).start()

        @pl.when(t == 3)
        def _():
            b_along_x()

        @pl.when(jnp.logical_and(t >= lag1, t < CHUNKS + lag1))
        def _():
            k = t - lag1
            first, second = legs(k, True), legs(k, False)
            for way in range(2):
                first[way].wait_recv()
                second[way].start()

        @pl.when(t == 6)
        def _():
            b_along_y()

        @pl.when(t == 9)
        def _():
            for copy in b_core():
                copy.start()

        @pl.when(t == 12)
        def _():
            other = 1 - c
            for yy in range(NY):
                drain(bfull.at[yy, other], bc_recv.at[yy])

        @pl.when(jnp.logical_and(t >= 12, t < 12 + CHUNKS // GROUP))
        def _():
            own_half(t - 12)

        @pl.when(t >= lag2)
        def _():
            k = t - lag2
            for copy in legs(k, False):
                copy.wait_recv()
            compute(k)

    drain(out_ref.at[pl.ds(0, (NJ - 1) * pairs)], c_recv)

    @pl.loop(0, CHUNKS)
    def _(k):
        drain(ybuf.at[k, pl.ds(0, NJ - 1)], y_send.at[k])
        for copy in legs(k, True) + legs(k, False):
            copy.wait_send()
        drain(cbuf.at[k, pl.ds(0, NJ - 1)], c_send.at[k])
        own_copy(k).wait()

    for way in range(2):
        for r in range(1, 5 - way):
            b_hop(r, way).wait_send()

    @pl.when(in_half)
    def _():
        for d in range(1, NX):
            drain(bfull.at[y, c, x % 2], bx_send.at[d - 1])

    for d in range(1, NY):
        drain(bfull.at[y, c], by_send.at[d - 1])
    for copy in b_core_copies():
        copy.wait_send()


def copy_out(src_ref, dst_ref):
    dst_ref[...] = src_ref[...]


def body(
    amplitudes, amplitude_map, integrals, integral_map, pair_list, occupied_energy, virtual_energy
):
    pair_count, rows, cols = amplitudes.shape
    q = pair_count // NJ // CHUNKS
    vmem = pl.BlockSpec(memory_space=pltpu.VMEM)
    hbm = pl.BlockSpec(memory_space=pl.ANY)
    smem = pl.BlockSpec(memory_space=pltpu.SMEM)
    dma = pltpu.SemaphoreType.DMA
    block = pltpu.VMEM((CHUNKS, NJ, q, rows, cols), jnp.bfloat16)
    update = pl.pallas_call(
        kernel,
        out_shape=jax.ShapeDtypeStruct(amplitudes.shape, jnp.bfloat16),
        in_specs=[hbm, smem, hbm, smem, smem, smem, smem, vmem],
        out_specs=pl.BlockSpec(memory_space=pl.ANY),
        scratch_shapes=[
            pltpu.VMEM(amplitudes.shape, jnp.bfloat16),
            block,
            block,
            block,
            block,
            pltpu.VMEM((NZL, TILE, 256), jnp.bfloat16),
            pltpu.VMEM((NY, NC, 2, 256, NZL * TILE), jnp.bfloat16),
            pltpu.VMEM((4, CHUNKS, q * rows, 256), jnp.float32),
            pltpu.VMEM((TILE, 128), jnp.float32),
            dma((CHUNKS,)),
            dma((CHUNKS,)),
            dma((CHUNKS, 2)),
            dma((CHUNKS, 2)),
            dma((CHUNKS, 2)),
            dma((CHUNKS, 2)),
            dma((CHUNKS,)),
            dma,
            dma((CHUNKS,)),
            dma((7,)),
            dma((7,)),
            dma((NX - 1,)),
            dma((2,)),
            dma((NY - 1,)),
            dma((NY,)),
            dma((NY,)),
            dma((NY,)),
            dma((2,)),
        ],
        compiler_params=pltpu.CompilerParams(
            collective_id=0, has_side_effects=True, vmem_limit_bytes=60 * 1024 * 1024
        ),
        cost_estimate=pl.CostEstimate(
            flops=2 * 1024 * 2048 * 1024, bytes_accessed=8 * 1024 * 1024, transcendentals=0
        ),
    )(
        amplitudes,
        amplitude_map,
        integrals,
        integral_map,
        pair_list.T,
        occupied_energy,
        virtual_energy,
        virtual_energy.reshape(1, -1),
    )
    part = pl.BlockSpec((pair_count // 8, rows, cols), lambda i: (i, 0, 0))
    return pl.pallas_call(
        copy_out,
        grid=(8,),
        out_shape=jax.ShapeDtypeStruct(amplitudes.shape, jnp.bfloat16),
        in_specs=[part],
        out_specs=part,
        compiler_params=pltpu.CompilerParams(vmem_limit_bytes=60 * 1024 * 1024),
    )(update)


def solution(mesh):
    in_specs = (
        P(None, "blk", "grp"),
        P("blk", "grp"),
        P("blk", None),
        P("blk", None),
        P(),
        P(),
        P(),
    )
    out_specs = P(None, "blk", "grp")
    return jax.shard_map(body, mesh=mesh, in_specs=in_specs, out_specs=out_specs, check_vma=False)
```

```python
import jax
import jax.numpy as jnp
from jax import lax
from jax.experimental import pallas as pl
from jax.experimental.pallas import tpu as pltpu
from jax.sharding import PartitionSpec as P

MESH = pl.DeviceIdType.MESH
TILE = 64
NX, NZ, NZL, NJ, NY, NC = 4, 16, 8, 8, 4, 2
CHUNKS = 16
AHEAD = 2
GROUP = 4
LEGS = (5, 3)


def drain(ref, sem):
    pltpu.make_async_copy(ref, ref, sem).wait()


def kernel(
    amp_hbm,
    amp_map_hbm,
    int_hbm,
    int_map_hbm,
    pair_hbm,
    occ_hbm,
    ve_hbm,
    ve_row_hbm,
    out_ref,
    amp_map_ref,
    int_map_ref,
    pair_ref,
    occ_ref,
    ve_smem,
    ve_row,
    masked,
    ybuf,
    relay,
    zbuf,
    cbuf,
    bline,
    bfull,
    own_acc,
    erow,
    y_send,
    y_recv,
    z_send,
    z_recv,
    f_send,
    f_recv,
    c_send,
    c_recv,
    own_sem,
    bz_send,
    bz_recv,
    bx_send,
    bx_recv,
    by_send,
    by_recv,
    bc_send,
    bc_recv,
    in_sem,
):
    b = lax.axis_index("blk")
    g = lax.axis_index("grp")
    x, zl = b // NZL, b % NZL
    h, j = g // NJ, g % NJ
    y, c = j // NC, j % NC
    z = h * NZL + zl
    pairs = amp_hbm.shape[1]
    q = pairs // CHUNKS
    half_cols = NJ * 128

    def at_z(zz):
        zz = (zz + NZ) % NZ
        return (x * NZL + zz % NZL, (zz // NZL) * NJ + j)

    def at_j(jj):
        return (b, h * NJ + jj)

    def at_x(xx):
        return (xx * NZL + zl, g)

    peers = [at_z(z + d) for d in (1, -1, 3, -3, 5, -5)]
    peers += [at_j((j + d) % NJ) for d in range(1, NJ)]
    peers += [at_x((x + d) % NX) for d in range(1, NX)]
    barrier = pltpu.get_barrier_semaphore()
    for peer in peers:
        pl.semaphore_signal(barrier, inc=1, device_id=peer, device_id_type=MESH)

    first, rest = pl.ds(0, q), pl.ds(q, pairs - q)
    loads = [
        pltpu.make_async_copy(src, dst, in_sem.at[i])
        for i, (src, dst) in enumerate(
            [
                (amp_map_hbm, amp_map_ref),
                (amp_hbm.at[:, first], masked.at[:, first]),
                (int_map_hbm, int_map_ref),
                (int_hbm.at[:, pl.ds(pl.multiple_of(j * 256, 128), 256)], bline.at[zl]),
                (amp_hbm.at[:, rest], masked.at[:, rest]),
                (pair_hbm, pair_ref),
                (occ_hbm, occ_ref),
                (ve_hbm, ve_smem),
                (ve_row_hbm, ve_row),
            ]
        )
    ]
    for load in loads:
        load.start()

    lane = lax.broadcasted_iota(jnp.int32, (1, 128), 1)

    def lane_mask(left, right):
        left, right = left.astype(jnp.float32), right.astype(jnp.float32)
        return jnp.where(lane < TILE, left, right).astype(jnp.bfloat16)

    loads[0].wait()
    amp_mask = lane_mask(amp_map_ref[0, 0], amp_map_ref[0, 1])

    def mask_chunk(k):
        for p in range(q):
            masked[:, k * q + p] = masked[:, k * q + p] * amp_mask[None]
            ybuf[k, j, p] = masked[j, k * q + p]

    loads[1].wait()
    mask_chunk(0)
    pl.semaphore_wait(barrier, len(peers))

    def send_chunk(k):
        for d in range(1, NJ):
            jj = (j + d) % NJ
            pltpu.make_async_remote_copy(
                src_ref=masked.at[jj, pl.ds(k * q, q)],
                dst_ref=ybuf.at[k, j],
                send_sem=y_send.at[k],
                recv_sem=y_recv.at[k],
                device_id=at_j(jj),
                device_id_type=MESH,
            ).start()

    send_chunk(0)
    loads[2].wait()
    loads[3].wait()
    for half in range(2):
        tile = 4 * j + 2 * half
        cols = slice(half * 128, half * 128 + 128)
        int_mask = lane_mask(int_map_ref[0, tile], int_map_ref[0, tile + 1])
        bline[zl, :, cols] = bline[zl, :, cols] * int_mask

    def b_hop(r, way):
        step = 1 if way == 0 else -1
        slot = (z - step * (r - 1) + NZ) % NZL
        return pltpu.make_async_remote_copy(
            src_ref=bline.at[slot],
            dst_ref=bline.at[slot],
            send_sem=bz_send.at[4 * way + r - 1],
            recv_sem=bz_recv.at[4 * way + r - 1],
            device_id=at_z(z + step),
            device_id_type=MESH,
        )

    def b_arrived(r, way):
        step = 1 if way == 0 else -1
        drain(bline.at[(z - step * r + NZ) % NZL], bz_recv.at[4 * way + r - 1])

    for way in range(2):
        b_hop(1, way).start()
    loads[4].wait()
    for k in range(1, AHEAD):
        mask_chunk(k)
        send_chunk(k)

    def legs(k, first):
        src, dst = (ybuf, relay) if first else (relay, zbuf)
        hops = LEGS[0] if first else LEGS[1]
        ssem, rsem = (z_send, z_recv) if first else (f_send, f_recv)
        return [
            pltpu.make_async_remote_copy(
                src_ref=src.at[k, pl.ds(4 * way, 4)],
                dst_ref=dst.at[k, pl.ds(4 * way, 4)],
                send_sem=ssem.at[k, way],
                recv_sem=rsem.at[k, way],
                device_id=at_z(z + (hops if way == 0 else -hops)),
                device_id_type=MESH,
            )
            for way in range(2)
        ]

    in_half = x // 2 == h

    def b_along_x():
        b_arrived(4, 0)

        @pl.when(in_half)
        def _():
            bfull[y, c, x % 2] = bline[...].reshape(NZL * TILE, 256).T
            for d in range(1, NX):
                pltpu.make_async_remote_copy(
                    src_ref=bfull.at[y, c, x % 2],
                    dst_ref=bfull.at[y, c, x % 2],
                    send_sem=bx_send.at[d - 1],
                    recv_sem=bx_recv.at[x % 2],
                    device_id=at_x((x + d) % NX),
                    device_id_type=MESH,
                ).start()

    def b_along_y():
        for xx in range(2):

            @pl.when(x != 2 * h + xx)
            def _():
                drain(bfull.at[y, c, xx], bx_recv.at[xx])

        for d in range(1, NY):
            pltpu.make_async_remote_copy(
                src_ref=bfull.at[y, c],
                dst_ref=bfull.at[y, c],
                send_sem=by_send.at[d - 1],
                recv_sem=by_recv.at[y],
                device_id=at_j(((y + d) % NY) * NC + c),
                device_id_type=MESH,
            ).start()

    def b_core():
        for d in range(1, NY):
            yy = (y + d) % NY
            drain(bfull.at[yy, c], by_recv.at[yy])
        return b_core_copies()

    def b_core_copies():
        return [
            pltpu.make_async_remote_copy(
                src_ref=bfull.at[yy, c],
                dst_ref=bfull.at[yy, c],
                send_sem=bc_send.at[yy],
                recv_sem=bc_recv.at[yy],
                device_id=at_j(y * NC + 1 - c),
                device_id_type=MESH,
            )
            for yy in range(NY)
        ]

    def weights(hh, i, n):
        cols = pl.ds(pl.multiple_of((n % 2) * 256, 256), 256)
        return bfull[2 * hh + i // 2, i % 2, n // 2, :, cols]

    def rows_of(buf, first, count, i):
        blocks = [
            buf[pl.ds(first, count), 2 * i + e].reshape(count * q * TILE, 128) for e in range(2)
        ]
        return jnp.concatenate(blocks, axis=1)

    def own_half(group):
        @pl.loop(0, 4)
        def _(n):
            acc = jnp.zeros((GROUP * q * TILE, 256), jnp.float32)
            for i in range(4):
                acc += jnp.dot(
                    rows_of(ybuf, group * GROUP, GROUP, i),
                    weights(h, i, n),
                    preferred_element_type=jnp.float32,
                )
            own_acc[n, pl.ds(group * GROUP, GROUP)] = acc.reshape(GROUP, q * TILE, 256)

    def compute(k):
        @pl.loop(0, 4)
        def _(step):
            n = (step + y) % 4
            acc = own_acc[n, k]
            for i in range(4):
                acc += jnp.dot(
                    rows_of(zbuf, k, 1, i),
                    weights(1 - h, i, n),
                    preferred_element_type=jnp.float32,
                )
            ladder = acc.astype(jnp.bfloat16).astype(jnp.float32)
            for e in range(2):
                start = pl.multiple_of(h * half_cols + n * 256 + e * 128, 128)
                virt = erow[...] + ve_row[:, pl.ds(start, 128)]
                for p in range(q):
                    pair = j * pairs + k * q + p
                    shift = occ_ref[pair_ref[0, pair]] + occ_ref[pair_ref[1, pair]]
                    block = ladder[p * TILE : (p + 1) * TILE, e * 128 : (e + 1) * 128]
                    cbuf[k, 2 * n + e, p] = (block / (virt - shift)).astype(jnp.bfloat16)

            for e in range(2):
                jj = 2 * n + e

                @pl.when(jj != j)
                def _():
                    pltpu.make_async_remote_copy(
                        src_ref=cbuf.at[k, jj],
                        dst_ref=out_ref.at[pl.ds(j * pairs + k * q, q)],
                        send_sem=c_send.at[k],
                        recv_sem=c_recv,
                        device_id=at_j(jj),
                        device_id_type=MESH,
                    ).start()

        own_copy(k).start()

    def own_copy(k):
        return pltpu.make_async_copy(
            cbuf.at[k, j], out_ref.at[pl.ds(j * pairs + k * q, q)], own_sem.at[k]
        )

    def sent(k):
        for copy in legs(k, False):
            copy.wait_send()
        drain(cbuf.at[k, pl.ds(0, NJ - 1)], c_send.at[k])
        own_copy(k).wait()

    def b_sent():
        for way in range(2):
            for r in range(1, 5 - way):
                b_hop(r, way).wait_send()

        @pl.when(in_half)
        def _():
            for d in range(1, NX):
                drain(bfull.at[y, c, x % 2], bx_send.at[d - 1])

        for d in range(1, NY):
            drain(bfull.at[y, c], by_send.at[d - 1])
        for copy in b_core_copies():
            copy.wait_send()

    lag1, lag2 = 4, 8

    @pl.loop(0, CHUNKS + lag2)
    def _(t):
        @pl.when(t < CHUNKS)
        def _():
            drain(ybuf.at[t, pl.ds(0, NJ - 1)], y_recv.at[t])
            for copy in legs(t, True):
                copy.start()

        @pl.when(t + AHEAD < CHUNKS)
        def _():
            mask_chunk(t + AHEAD)
            send_chunk(t + AHEAD)

        for r in range(1, 4):

            @pl.when(t == r - 1)
            def _():
                for way in range(2):
                    b_arrived(r, way)
                    if r + way < 4:
                        b_hop(r + 1, way).start()

        @pl.when(t == 3)
        def _():
            b_along_x()
            for load in loads[5:]:
                load.wait()

            @pl.loop(0, TILE)
            def _(r):
                erow[pl.ds(r, 1), :] = jnp.full((1, 128), ve_smem[b * TILE + r], jnp.float32)

        @pl.when(jnp.logical_and(t >= lag1, t < CHUNKS + lag1))
        def _():
            k = t - lag1
            first, second = legs(k, True), legs(k, False)
            for way in range(2):
                first[way].wait_recv()
                second[way].start()

        @pl.when(t == 5)
        def _():
            b_along_y()

        @pl.when(t == 6)
        def _():
            for copy in b_core():
                copy.start()

        @pl.when(t == lag2)
        def _():
            other = 1 - c
            for yy in range(NY):
                drain(bfull.at[yy, other], bc_recv.at[yy])
            b_sent()

        @pl.when(t >= lag2)
        def _():
            k = t - lag2

            @pl.when(k % GROUP == 0)
            def _():
                own_half(k // GROUP)

            drain(ybuf.at[k, pl.ds(0, NJ - 1)], y_send.at[k])
            for copy in legs(k, True):
                copy.wait_send()

            @pl.when(k > 0)
            def _():
                sent(k - 1)

            for copy in legs(k, False):
                copy.wait_recv()
            compute(k)

    sent(CHUNKS - 1)
    drain(out_ref.at[pl.ds(0, (NJ - 1) * pairs)], c_recv)


def body(
    amplitudes, amplitude_map, integrals, integral_map, pair_list, occupied_energy, virtual_energy
):
    pair_count, rows, cols = amplitudes.shape
    q = pair_count // NJ // CHUNKS
    hbm = pl.BlockSpec(memory_space=pl.ANY)
    dma = pltpu.SemaphoreType.DMA
    block = pltpu.VMEM((CHUNKS, NJ, q, rows, cols), jnp.bfloat16)
    return pl.pallas_call(
        kernel,
        out_shape=jax.ShapeDtypeStruct(amplitudes.shape, jnp.bfloat16),
        in_specs=[hbm] * 8,
        out_specs=pl.BlockSpec(memory_space=pl.ANY),
        scratch_shapes=[
            pltpu.SMEM(amplitude_map.shape, jnp.int32),
            pltpu.SMEM(integral_map.shape, jnp.int32),
            pltpu.SMEM((2, pair_count), jnp.int32),
            pltpu.SMEM(occupied_energy.shape, jnp.float32),
            pltpu.SMEM(virtual_energy.shape, jnp.float32),
            pltpu.VMEM((1, virtual_energy.size), jnp.float32),
            pltpu.VMEM((NJ, pair_count // NJ, rows, cols), jnp.bfloat16),
            block,
            block,
            block,
            block,
            pltpu.VMEM((NZL, TILE, 256), jnp.bfloat16),
            pltpu.VMEM((NY, NC, 2, 256, NZL * TILE), jnp.bfloat16),
            pltpu.VMEM((4, CHUNKS, q * rows, 256), jnp.float32),
            pltpu.VMEM((TILE, 128), jnp.float32),
            dma((CHUNKS,)),
            dma((CHUNKS,)),
            dma((CHUNKS, 2)),
            dma((CHUNKS, 2)),
            dma((CHUNKS, 2)),
            dma((CHUNKS, 2)),
            dma((CHUNKS,)),
            dma,
            dma((CHUNKS,)),
            dma((7,)),
            dma((7,)),
            dma((NX - 1,)),
            dma((2,)),
            dma((NY - 1,)),
            dma((NY,)),
            dma((NY,)),
            dma((NY,)),
            dma((9,)),
        ],
        compiler_params=pltpu.CompilerParams(
            collective_id=0, has_side_effects=True, vmem_limit_bytes=60 * 1024 * 1024
        ),
        cost_estimate=pl.CostEstimate(
            flops=2 * 1024 * 2048 * 1024, bytes_accessed=8 * 1024 * 1024, transcendentals=0
        ),
    )(
        amplitudes.reshape(NJ, pair_count // NJ, rows, cols),
        amplitude_map,
        integrals,
        integral_map,
        pair_list.T,
        occupied_energy,
        virtual_energy,
        virtual_energy.reshape(1, -1),
    )


def solution(mesh):
    in_specs = (
        P(None, "blk", "grp"),
        P("blk", "grp"),
        P("blk", None),
        P("blk", None),
        P(),
        P(),
        P(),
    )
    out_specs = P(None, "blk", "grp")
    return jax.shard_map(body, mesh=mesh, in_specs=in_specs, out_specs=out_specs, check_vma=False)
```

```python
import jax
import jax.numpy as jnp
from jax import lax
from jax.experimental import pallas as pl
from jax.experimental.pallas import tpu as pltpu
from jax.sharding import PartitionSpec as P

MESH = pl.DeviceIdType.MESH
TILE = 64
NX, NZ, NZL, NJ, NY, NC = 4, 16, 8, 8, 4, 2
CHUNKS = 16
AHEAD = 2
GROUP = 4
LEGS = (5, 3)


def drain(ref, sem):
    pltpu.make_async_copy(ref, ref, sem).wait()


def kernel(
    amp_hbm,
    amp_map_hbm,
    int_hbm,
    int_map_hbm,
    pair_hbm,
    occ_hbm,
    ve_hbm,
    ve_row_hbm,
    out_ref,
    amp_map_ref,
    int_map_ref,
    pair_ref,
    occ_ref,
    ve_smem,
    ve_row,
    masked,
    ybuf,
    relay,
    zbuf,
    cbuf,
    bline,
    bfull,
    own_acc,
    erow,
    y_send,
    y_recv,
    z_send,
    z_recv,
    f_send,
    f_recv,
    c_send,
    c_recv,
    own_sem,
    bz_send,
    bz_recv,
    bx_send,
    bx_recv,
    by_send,
    by_recv,
    bc_send,
    bc_recv,
    in_sem,
):
    b = lax.axis_index("blk")
    g = lax.axis_index("grp")
    x, zl = b // NZL, b % NZL
    h, j = g // NJ, g % NJ
    y, c = j // NC, j % NC
    z = h * NZL + zl
    pairs = amp_hbm.shape[1]
    q = pairs // CHUNKS
    half_cols = NJ * 128

    def at_z(zz):
        zz = (zz + NZ) % NZ
        return (x * NZL + zz % NZL, (zz // NZL) * NJ + j)

    def at_j(jj):
        return (b, h * NJ + jj)

    def at_x(xx):
        return (xx * NZL + zl, g)

    peers = [at_z(z + d) for d in (1, -1, 3, -3, 5, -5)]
    peers += [at_j((j + d) % NJ) for d in range(1, NJ)]
    peers += [at_x((x + d) % NX) for d in range(1, NX)]
    barrier = pltpu.get_barrier_semaphore()
    for peer in peers:
        pl.semaphore_signal(barrier, inc=1, device_id=peer, device_id_type=MESH)

    first, rest = pl.ds(0, q), pl.ds(q, pairs - q)
    loads = [
        pltpu.make_async_copy(src, dst, in_sem.at[i])
        for i, (src, dst) in enumerate(
            [
                (amp_map_hbm, amp_map_ref),
                (amp_hbm.at[:, first], masked.at[:, first]),
                (int_map_hbm, int_map_ref),
                (int_hbm.at[:, pl.ds(pl.multiple_of(j * 256, 128), 256)], bline.at[zl]),
                (amp_hbm.at[:, rest], masked.at[:, rest]),
                (pair_hbm, pair_ref),
                (occ_hbm, occ_ref),
                (ve_hbm, ve_smem),
                (ve_row_hbm, ve_row),
            ]
        )
    ]
    for load in loads:
        load.start()

    lane = lax.broadcasted_iota(jnp.int32, (1, 128), 1)

    def lane_mask(left, right):
        left, right = left.astype(jnp.float32), right.astype(jnp.float32)
        return jnp.where(lane < TILE, left, right).astype(jnp.bfloat16)

    loads[0].wait()
    amp_mask = lane_mask(amp_map_ref[0, 0], amp_map_ref[0, 1])

    def mask_chunk(k):
        for p in range(q):
            masked[:, k * q + p] = masked[:, k * q + p] * amp_mask[None]
            ybuf[k, j, p] = masked[j, k * q + p]

    loads[1].wait()
    mask_chunk(0)
    pl.semaphore_wait(barrier, len(peers))

    def send_chunk(k):
        for d in range(1, NJ):
            jj = (j + d) % NJ
            pltpu.make_async_remote_copy(
                src_ref=masked.at[jj, pl.ds(k * q, q)],
                dst_ref=ybuf.at[k, j],
                send_sem=y_send.at[k],
                recv_sem=y_recv.at[k],
                device_id=at_j(jj),
                device_id_type=MESH,
            ).start()

    send_chunk(0)
    loads[2].wait()
    loads[3].wait()
    for half in range(2):
        tile = 4 * j + 2 * half
        cols = slice(half * 128, half * 128 + 128)
        int_mask = lane_mask(int_map_ref[0, tile], int_map_ref[0, tile + 1])
        bline[zl, :, cols] = bline[zl, :, cols] * int_mask

    def b_hop(r, way):
        step = 1 if way == 0 else -1
        slot = (z - step * (r - 1) + NZ) % NZL
        return pltpu.make_async_remote_copy(
            src_ref=bline.at[slot],
            dst_ref=bline.at[slot],
            send_sem=bz_send.at[4 * way + r - 1],
            recv_sem=bz_recv.at[4 * way + r - 1],
            device_id=at_z(z + step),
            device_id_type=MESH,
        )

    def b_arrived(r, way):
        step = 1 if way == 0 else -1
        drain(bline.at[(z - step * r + NZ) % NZL], bz_recv.at[4 * way + r - 1])

    for way in range(2):
        b_hop(1, way).start()
    loads[4].wait()
    for k in range(1, AHEAD):
        mask_chunk(k)
        send_chunk(k)

    def legs(k, first):
        src, dst = (ybuf, relay) if first else (relay, zbuf)
        hops = LEGS[0] if first else LEGS[1]
        ssem, rsem = (z_send, z_recv) if first else (f_send, f_recv)
        return [
            pltpu.make_async_remote_copy(
                src_ref=src.at[k],
                dst_ref=dst.at[k],
                send_sem=ssem.at[k],
                recv_sem=rsem.at[k],
                device_id=at_z(z + hops * (1 - 2 * c)),
                device_id_type=MESH,
            )
        ]

    in_half = x // 2 == h

    def b_along_x():
        b_arrived(4, 0)

        @pl.when(in_half)
        def _():
            bfull[y, c, x % 2] = bline[...].reshape(NZL * TILE, 256).T
            for d in range(1, NX):
                pltpu.make_async_remote_copy(
                    src_ref=bfull.at[y, c, x % 2],
                    dst_ref=bfull.at[y, c, x % 2],
                    send_sem=bx_send.at[d - 1],
                    recv_sem=bx_recv.at[x % 2],
                    device_id=at_x((x + d) % NX),
                    device_id_type=MESH,
                ).start()

    def b_along_y():
        for xx in range(2):

            @pl.when(x != 2 * h + xx)
            def _():
                drain(bfull.at[y, c, xx], bx_recv.at[xx])

        for d in range(1, NY):
            pltpu.make_async_remote_copy(
                src_ref=bfull.at[y, c],
                dst_ref=bfull.at[y, c],
                send_sem=by_send.at[d - 1],
                recv_sem=by_recv.at[y],
                device_id=at_j(((y + d) % NY) * NC + c),
                device_id_type=MESH,
            ).start()

    def b_core():
        for d in range(1, NY):
            yy = (y + d) % NY
            drain(bfull.at[yy, c], by_recv.at[yy])
        return b_core_copies()

    def b_core_copies():
        return [
            pltpu.make_async_remote_copy(
                src_ref=bfull.at[yy, c],
                dst_ref=bfull.at[yy, c],
                send_sem=bc_send.at[yy],
                recv_sem=bc_recv.at[yy],
                device_id=at_j(y * NC + 1 - c),
                device_id_type=MESH,
            )
            for yy in range(NY)
        ]

    def weights(hh, i, n):
        cols = pl.ds(pl.multiple_of((n % 2) * 256, 256), 256)
        return bfull[2 * hh + i // 2, i % 2, n // 2, :, cols]

    def rows_of(buf, first, count, i):
        blocks = [
            buf[pl.ds(first, count), 2 * i + e].reshape(count * q * TILE, 128) for e in range(2)
        ]
        return jnp.concatenate(blocks, axis=1)

    def own_half(group):
        @pl.loop(0, 4)
        def _(n):
            acc = jnp.zeros((GROUP * q * TILE, 256), jnp.float32)
            for i in range(4):
                acc += jnp.dot(
                    rows_of(ybuf, group * GROUP, GROUP, i),
                    weights(h, i, n),
                    preferred_element_type=jnp.float32,
                )
            own_acc[n, pl.ds(group * GROUP, GROUP)] = acc.reshape(GROUP, q * TILE, 256)

    def compute(k):
        @pl.loop(0, 4)
        def _(step):
            n = (step + y) % 4
            acc = own_acc[n, k]
            for i in range(4):
                acc += jnp.dot(
                    rows_of(zbuf, k, 1, i),
                    weights(1 - h, i, n),
                    preferred_element_type=jnp.float32,
                )
            ladder = acc.astype(jnp.bfloat16).astype(jnp.float32)
            for e in range(2):
                start = pl.multiple_of(h * half_cols + n * 256 + e * 128, 128)
                virt = erow[...] + ve_row[:, pl.ds(start, 128)]
                for p in range(q):
                    pair = j * pairs + k * q + p
                    shift = occ_ref[pair_ref[0, pair]] + occ_ref[pair_ref[1, pair]]
                    block = ladder[p * TILE : (p + 1) * TILE, e * 128 : (e + 1) * 128]
                    cbuf[k, 2 * n + e, p] = (block / (virt - shift)).astype(jnp.bfloat16)

            for e in range(2):
                jj = 2 * n + e

                @pl.when(jj != j)
                def _():
                    pltpu.make_async_remote_copy(
                        src_ref=cbuf.at[k, jj],
                        dst_ref=out_ref.at[pl.ds(j * pairs + k * q, q)],
                        send_sem=c_send.at[k],
                        recv_sem=c_recv,
                        device_id=at_j(jj),
                        device_id_type=MESH,
                    ).start()

        own_copy(k).start()

    def own_copy(k):
        return pltpu.make_async_copy(
            cbuf.at[k, j], out_ref.at[pl.ds(j * pairs + k * q, q)], own_sem.at[k]
        )

    def sent(k):
        for copy in legs(k, False):
            copy.wait_send()
        drain(cbuf.at[k, pl.ds(0, NJ - 1)], c_send.at[k])
        own_copy(k).wait()

    def b_sent():
        for way in range(2):
            for r in range(1, 5 - way):
                b_hop(r, way).wait_send()

        @pl.when(in_half)
        def _():
            for d in range(1, NX):
                drain(bfull.at[y, c, x % 2], bx_send.at[d - 1])

        for d in range(1, NY):
            drain(bfull.at[y, c], by_send.at[d - 1])
        for copy in b_core_copies():
            copy.wait_send()

    lag1, lag2 = 4, 8

    @pl.loop(0, CHUNKS + lag2)
    def _(t):
        @pl.when(t < CHUNKS)
        def _():
            drain(ybuf.at[t, pl.ds(0, NJ - 1)], y_recv.at[t])
            for copy in legs(t, True):
                copy.start()

        @pl.when(t + AHEAD < CHUNKS)
        def _():
            mask_chunk(t + AHEAD)
            send_chunk(t + AHEAD)

        for r in range(1, 4):

            @pl.when(t == r - 1)
            def _():
                for way in range(2):
                    b_arrived(r, way)
                    if r + way < 4:
                        b_hop(r + 1, way).start()

        @pl.when(t == 3)
        def _():
            b_along_x()
            for load in loads[5:]:
                load.wait()

            @pl.loop(0, TILE)
            def _(r):
                erow[pl.ds(r, 1), :] = jnp.full((1, 128), ve_smem[b * TILE + r], jnp.float32)

        @pl.when(jnp.logical_and(t >= lag1, t < CHUNKS + lag1))
        def _():
            k = t - lag1
            for first, second in zip(legs(k, True), legs(k, False)):
                first.wait_recv()
                second.start()

        @pl.when(t == 5)
        def _():
            b_along_y()

        @pl.when(t == 6)
        def _():
            for copy in b_core():
                copy.start()

        @pl.when(t == lag2)
        def _():
            other = 1 - c
            for yy in range(NY):
                drain(bfull.at[yy, other], bc_recv.at[yy])
            b_sent()

        @pl.when(t >= lag2)
        def _():
            k = t - lag2

            @pl.when(k % GROUP == 0)
            def _():
                own_half(k // GROUP)

            drain(ybuf.at[k, pl.ds(0, NJ - 1)], y_send.at[k])
            for copy in legs(k, True):
                copy.wait_send()

            @pl.when(k > 0)
            def _():
                sent(k - 1)

            for copy in legs(k, False):
                copy.wait_recv()
            compute(k)

    sent(CHUNKS - 1)
    drain(out_ref.at[pl.ds(0, (NJ - 1) * pairs)], c_recv)


def body(
    amplitudes, amplitude_map, integrals, integral_map, pair_list, occupied_energy, virtual_energy
):
    pair_count, rows, cols = amplitudes.shape
    q = pair_count // NJ // CHUNKS
    hbm = pl.BlockSpec(memory_space=pl.ANY)
    dma = pltpu.SemaphoreType.DMA
    block = pltpu.VMEM((CHUNKS, NJ, q, rows, cols), jnp.bfloat16)
    return pl.pallas_call(
        kernel,
        out_shape=jax.ShapeDtypeStruct(amplitudes.shape, jnp.bfloat16),
        in_specs=[hbm] * 8,
        out_specs=pl.BlockSpec(memory_space=pl.ANY),
        scratch_shapes=[
            pltpu.SMEM(amplitude_map.shape, jnp.int32),
            pltpu.SMEM(integral_map.shape, jnp.int32),
            pltpu.SMEM((2, pair_count), jnp.int32),
            pltpu.SMEM(occupied_energy.shape, jnp.float32),
            pltpu.SMEM(virtual_energy.shape, jnp.float32),
            pltpu.VMEM((1, virtual_energy.size), jnp.float32),
            pltpu.VMEM((NJ, pair_count // NJ, rows, cols), jnp.bfloat16),
            block,
            block,
            block,
            block,
            pltpu.VMEM((NZL, TILE, 256), jnp.bfloat16),
            pltpu.VMEM((NY, NC, 2, 256, NZL * TILE), jnp.bfloat16),
            pltpu.VMEM((4, CHUNKS, q * rows, 256), jnp.float32),
            pltpu.VMEM((TILE, 128), jnp.float32),
            dma((CHUNKS,)),
            dma((CHUNKS,)),
            dma((CHUNKS,)),
            dma((CHUNKS,)),
            dma((CHUNKS,)),
            dma((CHUNKS,)),
            dma((CHUNKS,)),
            dma,
            dma((CHUNKS,)),
            dma((7,)),
            dma((7,)),
            dma((NX - 1,)),
            dma((2,)),
            dma((NY - 1,)),
            dma((NY,)),
            dma((NY,)),
            dma((NY,)),
            dma((9,)),
        ],
        compiler_params=pltpu.CompilerParams(
            collective_id=0, has_side_effects=True, vmem_limit_bytes=60 * 1024 * 1024
        ),
        cost_estimate=pl.CostEstimate(
            flops=2 * 1024 * 2048 * 1024, bytes_accessed=8 * 1024 * 1024, transcendentals=0
        ),
    )(
        amplitudes.reshape(NJ, pair_count // NJ, rows, cols),
        amplitude_map,
        integrals,
        integral_map,
        pair_list.T,
        occupied_energy,
        virtual_energy,
        virtual_energy.reshape(1, -1),
    )


def solution(mesh):
    in_specs = (
        P(None, "blk", "grp"),
        P("blk", "grp"),
        P("blk", None),
        P("blk", None),
        P(),
        P(),
        P(),
    )
    out_specs = P(None, "blk", "grp")
    return jax.shard_map(body, mesh=mesh, in_specs=in_specs, out_specs=out_specs, check_vma=False)
```

```python
import jax
import jax.numpy as jnp
from jax import lax
from jax.experimental import pallas as pl
from jax.experimental.pallas import tpu as pltpu
from jax.sharding import PartitionSpec as P

MESH = pl.DeviceIdType.MESH
TILE = 64
NX, NZ, NZL, NJ, NY, NC = 4, 16, 8, 8, 4, 2
CHUNKS = 16
AHEAD = 2
GROUP = 4
LEGS = (5, 3)


def drain(ref, sem):
    pltpu.make_async_copy(ref, ref, sem).wait()


def kernel(
    amp_hbm,
    amp_map_hbm,
    int_hbm,
    int_map_hbm,
    pair_hbm,
    occ_hbm,
    ve_hbm,
    ve_row_hbm,
    out_ref,
    amp_map_ref,
    int_map_ref,
    pair_ref,
    occ_ref,
    ve_smem,
    ve_row,
    masked,
    ybuf,
    relay,
    zbuf,
    cbuf,
    bline,
    bfull,
    own_acc,
    erow,
    y_send,
    y_recv,
    z_send,
    z_recv,
    f_send,
    f_recv,
    c_send,
    c_recv,
    own_sem,
    bz_send,
    bz_recv,
    bx_send,
    bx_recv,
    by_send,
    by_recv,
    bc_send,
    bc_recv,
    in_sem,
):
    b = lax.axis_index("blk")
    g = lax.axis_index("grp")
    x, zl = b // NZL, b % NZL
    h, j = g // NJ, g % NJ
    y, c = j // NC, j % NC
    z = h * NZL + zl
    pairs = amp_hbm.shape[1]
    q = pairs // CHUNKS
    half_cols = NJ * 128

    def at_z(zz):
        zz = (zz + NZ) % NZ
        return (x * NZL + zz % NZL, (zz // NZL) * NJ + j)

    def at_j(jj):
        return (b, h * NJ + jj)

    def at_x(xx):
        return (xx * NZL + zl, g)

    peers = [at_z(z + d) for d in (1, -1, 3, -3, 5, -5)]
    peers += [at_j((j + d) % NJ) for d in range(1, NJ)]
    peers += [at_x((x + d) % NX) for d in range(1, NX)]
    barrier = pltpu.get_barrier_semaphore()
    for peer in peers:
        pl.semaphore_signal(barrier, inc=1, device_id=peer, device_id_type=MESH)

    first, rest = pl.ds(0, q), pl.ds(q, pairs - q)
    loads = [
        pltpu.make_async_copy(src, dst, in_sem.at[i])
        for i, (src, dst) in enumerate(
            [
                (amp_map_hbm, amp_map_ref),
                (amp_hbm.at[:, first], masked.at[:, first]),
                (int_map_hbm, int_map_ref),
                (int_hbm.at[:, pl.ds(pl.multiple_of(j * 256, 128), 256)], bline.at[zl]),
                (amp_hbm.at[:, rest], masked.at[:, rest]),
                (pair_hbm, pair_ref),
                (occ_hbm, occ_ref),
                (ve_hbm, ve_smem),
                (ve_row_hbm, ve_row),
            ]
        )
    ]
    for load in loads:
        load.start()

    lane = lax.broadcasted_iota(jnp.int32, (1, 128), 1)

    def lane_mask(left, right):
        left, right = left.astype(jnp.float32), right.astype(jnp.float32)
        return jnp.where(lane < TILE, left, right).astype(jnp.bfloat16)

    loads[0].wait()
    amp_mask = lane_mask(amp_map_ref[0, 0], amp_map_ref[0, 1])

    def mask_chunk(k):
        for p in range(q):
            masked[:, k * q + p] = masked[:, k * q + p] * amp_mask[None]
            ybuf[k, j, p] = masked[j, k * q + p]

    loads[1].wait()
    mask_chunk(0)
    pl.semaphore_wait(barrier, len(peers))

    def send_chunk(k):
        for d in range(1, NJ):
            jj = (j + d) % NJ
            pltpu.make_async_remote_copy(
                src_ref=masked.at[jj, pl.ds(k * q, q)],
                dst_ref=ybuf.at[k, j],
                send_sem=y_send.at[k],
                recv_sem=y_recv.at[k],
                device_id=at_j(jj),
                device_id_type=MESH,
            ).start()

    send_chunk(0)
    loads[2].wait()
    loads[3].wait()
    for half in range(2):
        tile = 4 * j + 2 * half
        cols = slice(half * 128, half * 128 + 128)
        int_mask = lane_mask(int_map_ref[0, tile], int_map_ref[0, tile + 1])
        bline[zl, :, cols] = bline[zl, :, cols] * int_mask

    def b_hop(r, way):
        step = 1 if way == 0 else -1
        slot = (z - step * (r - 1) + NZ) % NZL
        return pltpu.make_async_remote_copy(
            src_ref=bline.at[slot],
            dst_ref=bline.at[slot],
            send_sem=bz_send.at[4 * way + r - 1],
            recv_sem=bz_recv.at[4 * way + r - 1],
            device_id=at_z(z + step),
            device_id_type=MESH,
        )

    def b_arrived(r, way):
        step = 1 if way == 0 else -1
        drain(bline.at[(z - step * r + NZ) % NZL], bz_recv.at[4 * way + r - 1])

    for way in range(2):
        b_hop(1, way).start()
    loads[4].wait()
    for k in range(1, AHEAD):
        mask_chunk(k)
        send_chunk(k)

    def legs(k, first):
        src, dst = (ybuf, relay) if first else (relay, zbuf)
        hops = LEGS[0] if first else LEGS[1]
        ssem, rsem = (z_send, z_recv) if first else (f_send, f_recv)
        return [
            pltpu.make_async_remote_copy(
                src_ref=src.at[k],
                dst_ref=dst.at[k],
                send_sem=ssem.at[k],
                recv_sem=rsem.at[k],
                device_id=at_z(z + hops * (1 - 2 * c)),
                device_id_type=MESH,
            )
        ]

    in_half = x // 2 == h

    def b_along_x():
        b_arrived(4, 0)

        @pl.when(in_half)
        def _():
            bfull[y, c, x % 2] = bline[...].reshape(NZL * TILE, 256).T
            for d in range(1, NX):
                pltpu.make_async_remote_copy(
                    src_ref=bfull.at[y, c, x % 2],
                    dst_ref=bfull.at[y, c, x % 2],
                    send_sem=bx_send.at[d - 1],
                    recv_sem=bx_recv.at[x % 2],
                    device_id=at_x((x + d) % NX),
                    device_id_type=MESH,
                ).start()

    def b_along_y():
        for xx in range(2):

            @pl.when(x != 2 * h + xx)
            def _():
                drain(bfull.at[y, c, xx], bx_recv.at[xx])

        for d in range(1, NY):
            pltpu.make_async_remote_copy(
                src_ref=bfull.at[y, c],
                dst_ref=bfull.at[y, c],
                send_sem=by_send.at[d - 1],
                recv_sem=by_recv.at[y],
                device_id=at_j(((y + d) % NY) * NC + c),
                device_id_type=MESH,
            ).start()

    def b_core():
        for d in range(1, NY):
            yy = (y + d) % NY
            drain(bfull.at[yy, c], by_recv.at[yy])
        return b_core_copies()

    def b_core_copies():
        return [
            pltpu.make_async_remote_copy(
                src_ref=bfull.at[yy, c],
                dst_ref=bfull.at[yy, c],
                send_sem=bc_send.at[yy],
                recv_sem=bc_recv.at[yy],
                device_id=at_j(y * NC + 1 - c),
                device_id_type=MESH,
            )
            for yy in range(NY)
        ]

    def weights(hh, i, n):
        cols = pl.ds(pl.multiple_of((n % 2) * 256, 256), 256)
        return bfull[2 * hh + i // 2, i % 2, n // 2, :, cols]

    def rows_of(buf, first, count, i):
        blocks = [
            buf[pl.ds(first, count), 2 * i + e].reshape(count * q * TILE, 128) for e in range(2)
        ]
        return jnp.concatenate(blocks, axis=1)

    def own_half(group):
        @pl.loop(0, 4)
        def _(n):
            acc = jnp.zeros((GROUP * q * TILE, 256), jnp.float32)
            for i in range(4):
                acc += jnp.dot(
                    rows_of(ybuf, group * GROUP, GROUP, i),
                    weights(h, i, n),
                    preferred_element_type=jnp.float32,
                )
            own_acc[n, pl.ds(group * GROUP, GROUP)] = acc.reshape(GROUP, q * TILE, 256)

    def compute(k):
        @pl.loop(0, 4)
        def _(step):
            n = (step + y) % 4
            acc = own_acc[n, k]
            for i in range(4):
                acc += jnp.dot(
                    rows_of(zbuf, k, 1, i),
                    weights(1 - h, i, n),
                    preferred_element_type=jnp.float32,
                )
            ladder = acc.astype(jnp.bfloat16).astype(jnp.float32)
            for e in range(2):
                start = pl.multiple_of(h * half_cols + n * 256 + e * 128, 128)
                virt = erow[...] + ve_row[:, pl.ds(start, 128)]
                for p in range(q):
                    pair = j * pairs + k * q + p
                    shift = occ_ref[pair_ref[0, pair]] + occ_ref[pair_ref[1, pair]]
                    block = ladder[p * TILE : (p + 1) * TILE, e * 128 : (e + 1) * 128]
                    cbuf[k, 2 * n + e, p] = (block / (virt - shift)).astype(jnp.bfloat16)

            for e in range(2):
                jj = 2 * n + e

                @pl.when(jj != j)
                def _():
                    pltpu.make_async_remote_copy(
                        src_ref=cbuf.at[k, jj],
                        dst_ref=out_ref.at[pl.ds(j * pairs + k * q, q)],
                        send_sem=c_send.at[k],
                        recv_sem=c_recv,
                        device_id=at_j(jj),
                        device_id_type=MESH,
                    ).start()

        own_copy(k).start()

    def own_copy(k):
        return pltpu.make_async_copy(
            cbuf.at[k, j], out_ref.at[pl.ds(j * pairs + k * q, q)], own_sem.at[k]
        )

    def sent(k):
        for copy in legs(k, False):
            copy.wait_send()
        drain(cbuf.at[k, pl.ds(0, NJ - 1)], c_send.at[k])
        own_copy(k).wait()

    def b_sent():
        for way in range(2):
            for r in range(1, 5 - way):
                b_hop(r, way).wait_send()

        @pl.when(in_half)
        def _():
            for d in range(1, NX):
                drain(bfull.at[y, c, x % 2], bx_send.at[d - 1])

        for d in range(1, NY):
            drain(bfull.at[y, c], by_send.at[d - 1])
        for copy in b_core_copies():
            copy.wait_send()

    def finish(k):
        drain(ybuf.at[k, pl.ds(0, NJ - 1)], y_send.at[k])
        for copy in legs(k, True):
            copy.wait_send()

        @pl.when(k > 0)
        def _():
            sent(k - 1)

        for copy in legs(k, False):
            copy.wait_recv()
        compute(k)

    lag1, lag2, start = 4, 8, 12

    @pl.loop(0, CHUNKS + lag2)
    def _(t):
        @pl.when(t < CHUNKS)
        def _():
            drain(ybuf.at[t, pl.ds(0, NJ - 1)], y_recv.at[t])
            for copy in legs(t, True):
                copy.start()

        for e in range(2):
            ahead = AHEAD + 2 * t + e

            @pl.when(ahead < CHUNKS)
            def _():
                mask_chunk(ahead)
                send_chunk(ahead)

        @pl.when(jnp.logical_and(t >= lag1, t < CHUNKS + lag1))
        def _():
            k = t - lag1
            for first, second in zip(legs(k, True), legs(k, False)):
                first.wait_recv()
                second.start()

        for r in range(1, 4):

            @pl.when(t == lag1 + r - 1)
            def _():
                for way in range(2):
                    b_arrived(r, way)
                    if r + way < 4:
                        b_hop(r + 1, way).start()

        @pl.when(t == 7)
        def _():
            b_along_x()
            for load in loads[5:]:
                load.wait()

            @pl.loop(0, TILE)
            def _(r):
                erow[pl.ds(r, 1), :] = jnp.full((1, 128), ve_smem[b * TILE + r], jnp.float32)

        @pl.when(t == 9)
        def _():
            b_along_y()

        @pl.when(t == 11)
        def _():
            for copy in b_core():
                copy.start()

        @pl.when(t == start)
        def _():
            other = 1 - c
            for yy in range(NY):
                drain(bfull.at[yy, other], bc_recv.at[yy])
            b_sent()

        @pl.when(jnp.logical_and(t >= start, t < start + CHUNKS // GROUP))
        def _():
            own_half(t - start)

        @pl.when(jnp.logical_and(t >= start, t < 2 * start - lag2))
        def _():
            for e in range(2):
                finish(2 * (t - start) + e)

        @pl.when(t >= 2 * start - lag2)
        def _():
            finish(t - lag2)

    sent(CHUNKS - 1)
    drain(out_ref.at[pl.ds(0, (NJ - 1) * pairs)], c_recv)


def body(
    amplitudes, amplitude_map, integrals, integral_map, pair_list, occupied_energy, virtual_energy
):
    pair_count, rows, cols = amplitudes.shape
    q = pair_count // NJ // CHUNKS
    hbm = pl.BlockSpec(memory_space=pl.ANY)
    dma = pltpu.SemaphoreType.DMA
    block = pltpu.VMEM((CHUNKS, NJ, q, rows, cols), jnp.bfloat16)
    return pl.pallas_call(
        kernel,
        out_shape=jax.ShapeDtypeStruct(amplitudes.shape, jnp.bfloat16),
        in_specs=[hbm] * 8,
        out_specs=pl.BlockSpec(memory_space=pl.ANY),
        scratch_shapes=[
            pltpu.SMEM(amplitude_map.shape, jnp.int32),
            pltpu.SMEM(integral_map.shape, jnp.int32),
            pltpu.SMEM((2, pair_count), jnp.int32),
            pltpu.SMEM(occupied_energy.shape, jnp.float32),
            pltpu.SMEM(virtual_energy.shape, jnp.float32),
            pltpu.VMEM((1, virtual_energy.size), jnp.float32),
            pltpu.VMEM((NJ, pair_count // NJ, rows, cols), jnp.bfloat16),
            block,
            block,
            block,
            block,
            pltpu.VMEM((NZL, TILE, 256), jnp.bfloat16),
            pltpu.VMEM((NY, NC, 2, 256, NZL * TILE), jnp.bfloat16),
            pltpu.VMEM((4, CHUNKS, q * rows, 256), jnp.float32),
            pltpu.VMEM((TILE, 128), jnp.float32),
            dma((CHUNKS,)),
            dma((CHUNKS,)),
            dma((CHUNKS,)),
            dma((CHUNKS,)),
            dma((CHUNKS,)),
            dma((CHUNKS,)),
            dma((CHUNKS,)),
            dma,
            dma((CHUNKS,)),
            dma((7,)),
            dma((7,)),
            dma((NX - 1,)),
            dma((2,)),
            dma((NY - 1,)),
            dma((NY,)),
            dma((NY,)),
            dma((NY,)),
            dma((9,)),
        ],
        compiler_params=pltpu.CompilerParams(
            collective_id=0, has_side_effects=True, vmem_limit_bytes=60 * 1024 * 1024
        ),
        cost_estimate=pl.CostEstimate(
            flops=2 * 1024 * 2048 * 1024, bytes_accessed=8 * 1024 * 1024, transcendentals=0
        ),
    )(
        amplitudes.reshape(NJ, pair_count // NJ, rows, cols),
        amplitude_map,
        integrals,
        integral_map,
        pair_list.T,
        occupied_energy,
        virtual_energy,
        virtual_energy.reshape(1, -1),
    )


def solution(mesh):
    in_specs = (
        P(None, "blk", "grp"),
        P("blk", "grp"),
        P("blk", None),
        P("blk", None),
        P(),
        P(),
        P(),
    )
    out_specs = P(None, "blk", "grp")
    return jax.shard_map(body, mesh=mesh, in_specs=in_specs, out_specs=out_specs, check_vma=False)
```

```python
import jax
import jax.numpy as jnp
from jax import lax
from jax.experimental import pallas as pl
from jax.experimental.pallas import tpu as pltpu
from jax.sharding import PartitionSpec as P

MESH = pl.DeviceIdType.MESH
TILE = 64
NX, NZ, NZL, NJ, NY, NC = 4, 16, 8, 8, 4, 2
CHUNKS = 16
AHEAD = 2
GROUP = 4
LEGS = (5, 3)


def drain(ref, sem):
    pltpu.make_async_copy(ref, ref, sem).wait()


def kernel(
    amp_hbm,
    amp_map_hbm,
    int_hbm,
    int_map_hbm,
    pair_hbm,
    occ_hbm,
    ve_hbm,
    ve_row_hbm,
    out_ref,
    amp_map_ref,
    int_map_ref,
    pair_ref,
    occ_ref,
    ve_smem,
    ve_row,
    masked,
    ybuf,
    relay,
    zbuf,
    cbuf,
    bline,
    bfull,
    own_acc,
    erow,
    y_send,
    y_recv,
    z_send,
    z_recv,
    f_send,
    f_recv,
    c_send,
    c_recv,
    own_sem,
    bz_send,
    bz_recv,
    bx_send,
    bx_recv,
    by_send,
    by_recv,
    bc_send,
    bc_recv,
    in_sem,
    hand_send,
    hand_recv,
):
    b = lax.axis_index("blk")
    g = lax.axis_index("grp")
    x, zl = b // NZL, b % NZL
    h, j = g // NJ, g % NJ
    y, c = j // NC, j % NC
    z = h * NZL + zl
    pairs = amp_hbm.shape[1]
    q = pairs // CHUNKS
    half_cols = NJ * 128

    def at_z(zz):
        zz = (zz + NZ) % NZ
        return (x * NZL + zz % NZL, (zz // NZL) * NJ + j)

    def at_j(jj):
        return (b, h * NJ + jj)

    def at_x(xx):
        return (xx * NZL + zl, g)

    peers = [at_z(z + d) for d in (1, -1, 3, -3, 5, -5)]
    peers += [at_j((j + d) % NJ) for d in range(1, NJ)]
    peers += [at_x((x + d) % NX) for d in range(1, NX)]
    barrier = pltpu.get_barrier_semaphore()
    for peer in peers:
        pl.semaphore_signal(barrier, inc=1, device_id=peer, device_id_type=MESH)

    first, rest = pl.ds(0, q), pl.ds(q, pairs - q)
    loads = [
        pltpu.make_async_copy(src, dst, in_sem.at[i])
        for i, (src, dst) in enumerate(
            [
                (amp_map_hbm, amp_map_ref),
                (amp_hbm.at[:, first], masked.at[:, first]),
                (int_map_hbm, int_map_ref),
                (int_hbm.at[:, pl.ds(pl.multiple_of(j * 256, 128), 256)], bline.at[zl]),
                (amp_hbm.at[:, rest], masked.at[:, rest]),
                (pair_hbm, pair_ref),
                (occ_hbm, occ_ref),
                (ve_hbm, ve_smem),
                (ve_row_hbm, ve_row),
            ]
        )
    ]
    for load in loads:
        load.start()

    lane = lax.broadcasted_iota(jnp.int32, (1, 128), 1)

    def lane_mask(left, right):
        left, right = left.astype(jnp.float32), right.astype(jnp.float32)
        return jnp.where(lane < TILE, left, right).astype(jnp.bfloat16)

    loads[0].wait()
    amp_mask = lane_mask(amp_map_ref[0, 0], amp_map_ref[0, 1])

    def mask_chunk(k):
        for p in range(q):
            masked[:, k * q + p] = masked[:, k * q + p] * amp_mask[None]
            ybuf[k, j, p] = masked[j, k * q + p]

    loads[1].wait()
    mask_chunk(0)
    pl.semaphore_wait(barrier, len(peers))

    def send_chunk(k):
        for d in range(1, NJ):
            jj = (j + d) % NJ
            pltpu.make_async_remote_copy(
                src_ref=masked.at[jj, pl.ds(k * q, q)],
                dst_ref=ybuf.at[k, j],
                send_sem=y_send.at[k],
                recv_sem=y_recv.at[k],
                device_id=at_j(jj),
                device_id_type=MESH,
            ).start()

    def legs(k, first):
        slot = (k + CHUNKS - 1) % CHUNKS + 1
        src, dst = (ybuf, relay) if first else (relay, zbuf)
        hops = LEGS[0] if first else LEGS[1]
        ssem, rsem = (z_send, z_recv) if first else (f_send, f_recv)
        return [
            pltpu.make_async_remote_copy(
                src_ref=src.at[k],
                dst_ref=dst.at[k if first else slot],
                send_sem=ssem.at[k],
                recv_sem=rsem.at[k],
                device_id=at_z(z + hops * (1 - 2 * c)),
                device_id_type=MESH,
            )
        ]

    def head_leg():
        return pltpu.make_async_remote_copy(
            src_ref=masked.at[:, pl.ds(0, q)],
            dst_ref=relay.at[0],
            send_sem=z_send.at[0],
            recv_sem=z_recv.at[0],
            device_id=at_z(z + LEGS[0] * (1 - 2 * c)),
            device_id_type=MESH,
        )

    def hand_on():
        for d in range(1, NJ):
            jj = (j + d) % NJ
            pltpu.make_async_remote_copy(
                src_ref=zbuf.at[CHUNKS, jj],
                dst_ref=zbuf.at[0, j],
                send_sem=hand_send,
                recv_sem=hand_recv,
                device_id=at_j(jj),
                device_id_type=MESH,
            ).start()
        zbuf[0, j] = zbuf[CHUNKS, j]

    head_leg().start()
    send_chunk(0)
    loads[2].wait()
    loads[3].wait()
    for half in range(2):
        tile = 4 * j + 2 * half
        cols = slice(half * 128, half * 128 + 128)
        int_mask = lane_mask(int_map_ref[0, tile], int_map_ref[0, tile + 1])
        bline[zl, :, cols] = bline[zl, :, cols] * int_mask

    def b_hop(r, way):
        step = 1 if way == 0 else -1
        slot = (z - step * (r - 1) + NZ) % NZL
        return pltpu.make_async_remote_copy(
            src_ref=bline.at[slot],
            dst_ref=bline.at[slot],
            send_sem=bz_send.at[4 * way + r - 1],
            recv_sem=bz_recv.at[4 * way + r - 1],
            device_id=at_z(z + step),
            device_id_type=MESH,
        )

    def b_arrived(r, way):
        step = 1 if way == 0 else -1
        drain(bline.at[(z - step * r + NZ) % NZL], bz_recv.at[4 * way + r - 1])

    for way in range(2):
        b_hop(1, way).start()
    loads[4].wait()
    for k in range(1, AHEAD):
        mask_chunk(k)
        send_chunk(k)

    in_half = x // 2 == h

    def b_along_x():
        b_arrived(4, 0)

        @pl.when(in_half)
        def _():
            bfull[y, c, x % 2] = bline[...].reshape(NZL * TILE, 256).T
            for d in range(1, NX):
                pltpu.make_async_remote_copy(
                    src_ref=bfull.at[y, c, x % 2],
                    dst_ref=bfull.at[y, c, x % 2],
                    send_sem=bx_send.at[d - 1],
                    recv_sem=bx_recv.at[x % 2],
                    device_id=at_x((x + d) % NX),
                    device_id_type=MESH,
                ).start()

    def b_along_y():
        for xx in range(2):

            @pl.when(x != 2 * h + xx)
            def _():
                drain(bfull.at[y, c, xx], bx_recv.at[xx])

        for d in range(1, NY):
            pltpu.make_async_remote_copy(
                src_ref=bfull.at[y, c],
                dst_ref=bfull.at[y, c],
                send_sem=by_send.at[d - 1],
                recv_sem=by_recv.at[y],
                device_id=at_j(((y + d) % NY) * NC + c),
                device_id_type=MESH,
            ).start()

    def b_core():
        for d in range(1, NY):
            yy = (y + d) % NY
            drain(bfull.at[yy, c], by_recv.at[yy])
        return b_core_copies()

    def b_core_copies():
        return [
            pltpu.make_async_remote_copy(
                src_ref=bfull.at[yy, c],
                dst_ref=bfull.at[yy, c],
                send_sem=bc_send.at[yy],
                recv_sem=bc_recv.at[yy],
                device_id=at_j(y * NC + 1 - c),
                device_id_type=MESH,
            )
            for yy in range(NY)
        ]

    def weights(hh, i, n):
        cols = pl.ds(pl.multiple_of((n % 2) * 256, 256), 256)
        return bfull[2 * hh + i // 2, i % 2, n // 2, :, cols]

    def rows_of(buf, first, count, i):
        blocks = [
            buf[pl.ds(first, count), 2 * i + e].reshape(count * q * TILE, 128) for e in range(2)
        ]
        return jnp.concatenate(blocks, axis=1)

    def own_half(group):
        @pl.loop(0, 4)
        def _(n):
            acc = jnp.zeros((GROUP * q * TILE, 256), jnp.float32)
            for i in range(4):
                acc += jnp.dot(
                    rows_of(ybuf, group * GROUP, GROUP, i),
                    weights(h, i, n),
                    preferred_element_type=jnp.float32,
                )
            own_acc[n, pl.ds(group * GROUP, GROUP)] = acc.reshape(GROUP, q * TILE, 256)

    def compute(k):
        @pl.loop(0, 4)
        def _(step):
            n = (step + y) % 4
            acc = own_acc[n, k]
            for i in range(4):
                acc += jnp.dot(
                    rows_of(zbuf, k, 1, i),
                    weights(1 - h, i, n),
                    preferred_element_type=jnp.float32,
                )
            ladder = acc.astype(jnp.bfloat16).astype(jnp.float32)
            for e in range(2):
                start = pl.multiple_of(h * half_cols + n * 256 + e * 128, 128)
                virt = erow[...] + ve_row[:, pl.ds(start, 128)]
                for p in range(q):
                    pair = j * pairs + k * q + p
                    shift = occ_ref[pair_ref[0, pair]] + occ_ref[pair_ref[1, pair]]
                    block = ladder[p * TILE : (p + 1) * TILE, e * 128 : (e + 1) * 128]
                    cbuf[k, 2 * n + e, p] = (block / (virt - shift)).astype(jnp.bfloat16)

            for e in range(2):
                jj = 2 * n + e

                @pl.when(jj != j)
                def _():
                    pltpu.make_async_remote_copy(
                        src_ref=cbuf.at[k, jj],
                        dst_ref=out_ref.at[pl.ds(j * pairs + k * q, q)],
                        send_sem=c_send.at[k],
                        recv_sem=c_recv,
                        device_id=at_j(jj),
                        device_id_type=MESH,
                    ).start()

        own_copy(k).start()

    def own_copy(k):
        return pltpu.make_async_copy(
            cbuf.at[k, j], out_ref.at[pl.ds(j * pairs + k * q, q)], own_sem.at[k]
        )

    def sent(k):
        for copy in legs(k, False):
            copy.wait_send()
        drain(cbuf.at[k, pl.ds(0, NJ - 1)], c_send.at[k])
        own_copy(k).wait()

    def b_sent():
        for way in range(2):
            for r in range(1, 5 - way):
                b_hop(r, way).wait_send()

        @pl.when(in_half)
        def _():
            for d in range(1, NX):
                drain(bfull.at[y, c, x % 2], bx_send.at[d - 1])

        for d in range(1, NY):
            drain(bfull.at[y, c], by_send.at[d - 1])
        for copy in b_core_copies():
            copy.wait_send()

    def finish(k):
        drain(ybuf.at[k, pl.ds(0, NJ - 1)], y_send.at[k])
        for copy in legs(k, True):
            copy.wait_send()

        @pl.when(k > 0)
        def _():
            sent(k - 1)

        @pl.when(k > 0)
        def _():
            for copy in legs(k, False):
                copy.wait_recv()

        compute(k)

    lag1, lag2, start = 4, 8, 12

    @pl.loop(0, CHUNKS + lag2)
    def _(t):
        @pl.when(t < CHUNKS)
        def _():
            drain(ybuf.at[t, pl.ds(0, NJ - 1)], y_recv.at[t])

            @pl.when(t > 0)
            def _():
                for copy in legs(t, True):
                    copy.start()

        for e in range(2):
            ahead = AHEAD + 2 * t + e

            @pl.when(ahead < CHUNKS)
            def _():
                mask_chunk(ahead)
                send_chunk(ahead)

        @pl.when(jnp.logical_and(t >= lag1, t < CHUNKS + lag1))
        def _():
            k = t - lag1
            for first, second in zip(legs(k, True), legs(k, False)):
                first.wait_recv()
                second.start()

        for r in range(1, 4):

            @pl.when(t == lag1 + r - 1)
            def _():
                for way in range(2):
                    b_arrived(r, way)
                    if r + way < 4:
                        b_hop(r + 1, way).start()

        @pl.when(t == 7)
        def _():
            b_along_x()
            for load in loads[5:]:
                load.wait()

            @pl.loop(0, TILE)
            def _(r):
                erow[pl.ds(r, 1), :] = jnp.full((1, 128), ve_smem[b * TILE + r], jnp.float32)

        @pl.when(t == lag2)
        def _():
            for copy in legs(0, False):
                copy.wait_recv()
            hand_on()

        @pl.when(t == 9)
        def _():
            b_along_y()

        @pl.when(t == 11)
        def _():
            for copy in b_core():
                copy.start()

        @pl.when(t == start)
        def _():
            other = 1 - c
            for yy in range(NY):
                drain(bfull.at[yy, other], bc_recv.at[yy])
            b_sent()
            drain(zbuf.at[0, pl.ds(0, NJ - 1)], hand_recv)
            drain(zbuf.at[0, pl.ds(0, NJ - 1)], hand_send)

        @pl.when(jnp.logical_and(t >= start, t < start + CHUNKS // GROUP))
        def _():
            own_half(t - start)

        @pl.when(jnp.logical_and(t >= start, t < 2 * start - lag2))
        def _():
            for e in range(2):
                finish(2 * (t - start) + e)

        @pl.when(t >= 2 * start - lag2)
        def _():
            finish(t - lag2)

    sent(CHUNKS - 1)
    drain(out_ref.at[pl.ds(0, (NJ - 1) * pairs)], c_recv)


def body(
    amplitudes, amplitude_map, integrals, integral_map, pair_list, occupied_energy, virtual_energy
):
    pair_count, rows, cols = amplitudes.shape
    q = pair_count // NJ // CHUNKS
    hbm = pl.BlockSpec(memory_space=pl.ANY)
    dma = pltpu.SemaphoreType.DMA
    block = pltpu.VMEM((CHUNKS, NJ, q, rows, cols), jnp.bfloat16)
    return pl.pallas_call(
        kernel,
        out_shape=jax.ShapeDtypeStruct(amplitudes.shape, jnp.bfloat16),
        in_specs=[hbm] * 8,
        out_specs=pl.BlockSpec(memory_space=pl.ANY),
        scratch_shapes=[
            pltpu.SMEM(amplitude_map.shape, jnp.int32),
            pltpu.SMEM(integral_map.shape, jnp.int32),
            pltpu.SMEM((2, pair_count), jnp.int32),
            pltpu.SMEM(occupied_energy.shape, jnp.float32),
            pltpu.SMEM(virtual_energy.shape, jnp.float32),
            pltpu.VMEM((1, virtual_energy.size), jnp.float32),
            pltpu.VMEM((NJ, pair_count // NJ, rows, cols), jnp.bfloat16),
            block,
            block,
            pltpu.VMEM((CHUNKS + 1, NJ, q, rows, cols), jnp.bfloat16),
            block,
            pltpu.VMEM((NZL, TILE, 256), jnp.bfloat16),
            pltpu.VMEM((NY, NC, 2, 256, NZL * TILE), jnp.bfloat16),
            pltpu.VMEM((4, CHUNKS, q * rows, 256), jnp.float32),
            pltpu.VMEM((TILE, 128), jnp.float32),
            dma((CHUNKS,)),
            dma((CHUNKS,)),
            dma((CHUNKS,)),
            dma((CHUNKS,)),
            dma((CHUNKS,)),
            dma((CHUNKS,)),
            dma((CHUNKS,)),
            dma,
            dma((CHUNKS,)),
            dma((7,)),
            dma((7,)),
            dma((NX - 1,)),
            dma((2,)),
            dma((NY - 1,)),
            dma((NY,)),
            dma((NY,)),
            dma((NY,)),
            dma((9,)),
            dma,
            dma,
        ],
        compiler_params=pltpu.CompilerParams(
            collective_id=0, has_side_effects=True, vmem_limit_bytes=60 * 1024 * 1024
        ),
        cost_estimate=pl.CostEstimate(
            flops=2 * 1024 * 2048 * 1024, bytes_accessed=8 * 1024 * 1024, transcendentals=0
        ),
    )(
        amplitudes.reshape(NJ, pair_count // NJ, rows, cols),
        amplitude_map,
        integrals,
        integral_map,
        pair_list.T,
        occupied_energy,
        virtual_energy,
        virtual_energy.reshape(1, -1),
    )


def solution(mesh):
    in_specs = (
        P(None, "blk", "grp"),
        P("blk", "grp"),
        P("blk", None),
        P("blk", None),
        P(),
        P(),
        P(),
    )
    out_specs = P(None, "blk", "grp")
    return jax.shard_map(body, mesh=mesh, in_specs=in_specs, out_specs=out_specs, check_vma=False)
```

```python
import jax
import jax.numpy as jnp
from jax import lax
from jax.experimental import pallas as pl
from jax.experimental.pallas import tpu as pltpu
from jax.sharding import PartitionSpec as P

MESH = pl.DeviceIdType.MESH
TILE = 64
NX, NZ, NZL, NJ, NY, NC = 4, 16, 8, 8, 4, 2
CHUNKS = 16
HEAD, AHEAD = 2, 4
GROUP = 4
LEGS = (5, 3)


def drain(ref, sem):
    pltpu.make_async_copy(ref, ref, sem).wait()


def kernel(
    amp_hbm,
    amp_map_hbm,
    int_hbm,
    int_map_hbm,
    pair_hbm,
    occ_hbm,
    ve_hbm,
    ve_row_hbm,
    out_ref,
    amp_map_ref,
    int_map_ref,
    pair_ref,
    occ_ref,
    ve_smem,
    ve_row,
    masked,
    ybuf,
    relay,
    zbuf,
    cbuf,
    bline,
    bfull,
    own_acc,
    erow,
    y_send,
    y_recv,
    z_send,
    z_recv,
    f_send,
    f_recv,
    c_send,
    c_recv,
    own_sem,
    bz_send,
    bz_recv,
    bx_send,
    bx_recv,
    by_send,
    by_recv,
    bc_send,
    bc_recv,
    in_sem,
    hand_send,
    hand_recv,
):
    b = lax.axis_index("blk")
    g = lax.axis_index("grp")
    x, zl = b // NZL, b % NZL
    h, j = g // NJ, g % NJ
    y, c = j // NC, j % NC
    z = h * NZL + zl
    pairs = amp_hbm.shape[1]
    q = pairs // CHUNKS
    half_cols = NJ * 128

    def at_z(zz):
        zz = (zz + NZ) % NZ
        return (x * NZL + zz % NZL, (zz // NZL) * NJ + j)

    def at_j(jj):
        return (b, h * NJ + jj)

    def at_x(xx):
        return (xx * NZL + zl, g)

    peers = [at_z(z + d) for d in (1, -1, 3, -3, 5, -5)]
    peers += [at_j((j + d) % NJ) for d in range(1, NJ)]
    peers += [at_x((x + d) % NX) for d in range(1, NX)]
    barrier = pltpu.get_barrier_semaphore()
    for peer in peers:
        pl.semaphore_signal(barrier, inc=1, device_id=peer, device_id_type=MESH)

    first, rest = pl.ds(0, HEAD * q), pl.ds(HEAD * q, pairs - HEAD * q)
    loads = [
        pltpu.make_async_copy(src, dst, in_sem.at[i])
        for i, (src, dst) in enumerate(
            [
                (amp_map_hbm, amp_map_ref),
                (amp_hbm.at[:, first], masked.at[:, first]),
                (int_map_hbm, int_map_ref),
                (int_hbm.at[:, pl.ds(pl.multiple_of(j * 256, 128), 256)], bline.at[zl]),
                (amp_hbm.at[:, rest], masked.at[:, rest]),
                (pair_hbm, pair_ref),
                (occ_hbm, occ_ref),
                (ve_hbm, ve_smem),
                (ve_row_hbm, ve_row),
            ]
        )
    ]
    for load in loads:
        load.start()

    lane = lax.broadcasted_iota(jnp.int32, (1, 128), 1)

    def lane_mask(left, right):
        left, right = left.astype(jnp.float32), right.astype(jnp.float32)
        return jnp.where(lane < TILE, left, right).astype(jnp.bfloat16)

    loads[0].wait()
    amp_mask = lane_mask(amp_map_ref[0, 0], amp_map_ref[0, 1])

    def mask_chunk(k):
        for p in range(q):
            masked[:, k * q + p] = masked[:, k * q + p] * amp_mask[None]
            ybuf[k, j, p] = masked[j, k * q + p]

    loads[1].wait()
    for k in range(HEAD):
        mask_chunk(k)
    pl.semaphore_wait(barrier, len(peers))

    def send_chunk(k):
        for d in range(1, NJ):
            jj = (j + d) % NJ
            pltpu.make_async_remote_copy(
                src_ref=masked.at[jj, pl.ds(k * q, q)],
                dst_ref=ybuf.at[k, j],
                send_sem=y_send.at[k],
                recv_sem=y_recv.at[k],
                device_id=at_j(jj),
                device_id_type=MESH,
            ).start()

    def legs(k, first):
        slot = (k + CHUNKS - HEAD) % CHUNKS + HEAD
        src, dst = (ybuf, relay) if first else (relay, zbuf)
        hops = LEGS[0] if first else LEGS[1]
        ssem, rsem = (z_send, z_recv) if first else (f_send, f_recv)
        return [
            pltpu.make_async_remote_copy(
                src_ref=src.at[k],
                dst_ref=dst.at[k if first else slot],
                send_sem=ssem.at[k],
                recv_sem=rsem.at[k],
                device_id=at_z(z + hops * (1 - 2 * c)),
                device_id_type=MESH,
            )
        ]

    def head_leg(k):
        return pltpu.make_async_remote_copy(
            src_ref=masked.at[:, pl.ds(k * q, q)],
            dst_ref=relay.at[k],
            send_sem=z_send.at[k],
            recv_sem=z_recv.at[k],
            device_id=at_z(z + LEGS[0] * (1 - 2 * c)),
            device_id_type=MESH,
        )

    def hand_on(k):
        for d in range(1, NJ):
            jj = (j + d) % NJ
            pltpu.make_async_remote_copy(
                src_ref=zbuf.at[CHUNKS + k, jj],
                dst_ref=zbuf.at[k, j],
                send_sem=hand_send.at[k],
                recv_sem=hand_recv.at[k],
                device_id=at_j(jj),
                device_id_type=MESH,
            ).start()
        zbuf[k, j] = zbuf[CHUNKS + k, j]

    for k in range(HEAD):
        head_leg(k).start()
    loads[4].wait()
    mask_chunk(HEAD)
    send_chunk(HEAD)
    loads[2].wait()
    loads[3].wait()
    for half in range(2):
        tile = 4 * j + 2 * half
        cols = slice(half * 128, half * 128 + 128)
        int_mask = lane_mask(int_map_ref[0, tile], int_map_ref[0, tile + 1])
        bline[zl, :, cols] = bline[zl, :, cols] * int_mask

    def b_hop(r, way):
        step = 1 if way == 0 else -1
        slot = (z - step * (r - 1) + NZ) % NZL
        return pltpu.make_async_remote_copy(
            src_ref=bline.at[slot],
            dst_ref=bline.at[slot],
            send_sem=bz_send.at[4 * way + r - 1],
            recv_sem=bz_recv.at[4 * way + r - 1],
            device_id=at_z(z + step),
            device_id_type=MESH,
        )

    def b_arrived(r, way):
        step = 1 if way == 0 else -1
        drain(bline.at[(z - step * r + NZ) % NZL], bz_recv.at[4 * way + r - 1])

    for way in range(2):
        b_hop(1, way).start()
    for k in range(HEAD + 1, AHEAD):
        mask_chunk(k)
        send_chunk(k)

    in_half = x // 2 == h

    def b_along_x():
        b_arrived(4, 0)

        @pl.when(in_half)
        def _():
            bfull[y, c, x % 2] = bline[...].reshape(NZL * TILE, 256).T
            for d in range(1, NX):
                pltpu.make_async_remote_copy(
                    src_ref=bfull.at[y, c, x % 2],
                    dst_ref=bfull.at[y, c, x % 2],
                    send_sem=bx_send.at[d - 1],
                    recv_sem=bx_recv.at[x % 2],
                    device_id=at_x((x + d) % NX),
                    device_id_type=MESH,
                ).start()

    def b_along_y():
        for xx in range(2):

            @pl.when(x != 2 * h + xx)
            def _():
                drain(bfull.at[y, c, xx], bx_recv.at[xx])

        for d in range(1, NY):
            pltpu.make_async_remote_copy(
                src_ref=bfull.at[y, c],
                dst_ref=bfull.at[y, c],
                send_sem=by_send.at[d - 1],
                recv_sem=by_recv.at[y],
                device_id=at_j(((y + d) % NY) * NC + c),
                device_id_type=MESH,
            ).start()

    def b_core():
        for d in range(1, NY):
            yy = (y + d) % NY
            drain(bfull.at[yy, c], by_recv.at[yy])
        return b_core_copies()

    def b_core_copies():
        return [
            pltpu.make_async_remote_copy(
                src_ref=bfull.at[yy, c],
                dst_ref=bfull.at[yy, c],
                send_sem=bc_send.at[yy],
                recv_sem=bc_recv.at[yy],
                device_id=at_j(y * NC + 1 - c),
                device_id_type=MESH,
            )
            for yy in range(NY)
        ]

    def weights(hh, i, n):
        cols = pl.ds(pl.multiple_of((n % 2) * 256, 256), 256)
        return bfull[2 * hh + i // 2, i % 2, n // 2, :, cols]

    def rows_of(buf, first, count, i):
        blocks = [
            buf[pl.ds(first, count), 2 * i + e].reshape(count * q * TILE, 128) for e in range(2)
        ]
        return jnp.concatenate(blocks, axis=1)

    def own_half(group):
        @pl.loop(0, 4)
        def _(n):
            acc = jnp.zeros((GROUP * q * TILE, 256), jnp.float32)
            for i in range(4):
                acc += jnp.dot(
                    rows_of(ybuf, group * GROUP, GROUP, i),
                    weights(h, i, n),
                    preferred_element_type=jnp.float32,
                )
            own_acc[n, pl.ds(group * GROUP, GROUP)] = acc.reshape(GROUP, q * TILE, 256)

    def compute(k):
        @pl.loop(0, 4)
        def _(step):
            n = (step + y) % 4
            acc = own_acc[n, k]
            for i in range(4):
                acc += jnp.dot(
                    rows_of(zbuf, k, 1, i),
                    weights(1 - h, i, n),
                    preferred_element_type=jnp.float32,
                )
            ladder = acc.astype(jnp.bfloat16).astype(jnp.float32)
            for e in range(2):
                start = pl.multiple_of(h * half_cols + n * 256 + e * 128, 128)
                virt = erow[...] + ve_row[:, pl.ds(start, 128)]
                for p in range(q):
                    pair = j * pairs + k * q + p
                    shift = occ_ref[pair_ref[0, pair]] + occ_ref[pair_ref[1, pair]]
                    block = ladder[p * TILE : (p + 1) * TILE, e * 128 : (e + 1) * 128]
                    cbuf[k, 2 * n + e, p] = (block / (virt - shift)).astype(jnp.bfloat16)

            for e in range(2):
                jj = 2 * n + e

                @pl.when(jj != j)
                def _():
                    pltpu.make_async_remote_copy(
                        src_ref=cbuf.at[k, jj],
                        dst_ref=out_ref.at[pl.ds(j * pairs + k * q, q)],
                        send_sem=c_send.at[k],
                        recv_sem=c_recv,
                        device_id=at_j(jj),
                        device_id_type=MESH,
                    ).start()

        own_copy(k).start()

    def own_copy(k):
        return pltpu.make_async_copy(
            cbuf.at[k, j], out_ref.at[pl.ds(j * pairs + k * q, q)], own_sem.at[k]
        )

    def sent(k):
        for copy in legs(k, False):
            copy.wait_send()
        drain(cbuf.at[k, pl.ds(0, NJ - 1)], c_send.at[k])
        own_copy(k).wait()

    def b_sent():
        for way in range(2):
            for r in range(1, 5 - way):
                b_hop(r, way).wait_send()

        @pl.when(in_half)
        def _():
            for d in range(1, NX):
                drain(bfull.at[y, c, x % 2], bx_send.at[d - 1])

        for d in range(1, NY):
            drain(bfull.at[y, c], by_send.at[d - 1])
        for copy in b_core_copies():
            copy.wait_send()

    def finish(k):
        drain(ybuf.at[k, pl.ds(0, NJ - 1)], y_send.at[k])
        for copy in legs(k, True):
            copy.wait_send()

        @pl.when(k > 0)
        def _():
            sent(k - 1)

        @pl.when(k >= HEAD)
        def _():
            for copy in legs(k, False):
                copy.wait_recv()

        compute(k)

    lag1, lag2, start = 4, 8, 12

    @pl.loop(0, CHUNKS + lag2)
    def _(t):
        @pl.when(jnp.logical_and(t >= HEAD, t < CHUNKS))
        def _():
            drain(ybuf.at[t, pl.ds(0, NJ - 1)], y_recv.at[t])
            for copy in legs(t, True):
                copy.start()

        for e in range(2):
            ahead = AHEAD + 2 * t + e

            @pl.when(ahead < CHUNKS)
            def _():
                mask_chunk(ahead)
                send_chunk(ahead)

        @pl.when(jnp.logical_and(t >= lag1, t < CHUNKS + lag1))
        def _():
            k = t - lag1
            for first, second in zip(legs(k, True), legs(k, False)):
                first.wait_recv()
                second.start()

        @pl.when(t == 7)
        def _():
            for k in range(HEAD):
                send_chunk(k)

        for r in range(1, 4):

            @pl.when(t == lag1 + r - 1)
            def _():
                for way in range(2):
                    b_arrived(r, way)
                    if r + way < 4:
                        b_hop(r + 1, way).start()

        @pl.when(t == 7)
        def _():
            b_along_x()
            for load in loads[5:]:
                load.wait()

            @pl.loop(0, TILE)
            def _(r):
                erow[pl.ds(r, 1), :] = jnp.full((1, 128), ve_smem[b * TILE + r], jnp.float32)

        @pl.when(jnp.logical_and(t >= lag2, t < lag2 + HEAD))
        def _():
            for copy in legs(t - lag2, False):
                copy.wait_recv()
            hand_on(t - lag2)

        @pl.when(t == 9)
        def _():
            b_along_y()

        @pl.when(t == 11)
        def _():
            for copy in b_core():
                copy.start()

        @pl.when(t == start)
        def _():
            other = 1 - c
            for yy in range(NY):
                drain(bfull.at[yy, other], bc_recv.at[yy])
            b_sent()
            for k in range(HEAD):
                drain(ybuf.at[k, pl.ds(0, NJ - 1)], y_recv.at[k])
                drain(zbuf.at[k, pl.ds(0, NJ - 1)], hand_recv.at[k])
                drain(zbuf.at[k, pl.ds(0, NJ - 1)], hand_send.at[k])

        @pl.when(jnp.logical_and(t >= start, t < start + CHUNKS // GROUP))
        def _():
            own_half(t - start)

        @pl.when(jnp.logical_and(t >= start, t < 2 * start - lag2))
        def _():
            for e in range(2):
                finish(2 * (t - start) + e)

        @pl.when(t >= 2 * start - lag2)
        def _():
            finish(t - lag2)

    sent(CHUNKS - 1)
    drain(out_ref.at[pl.ds(0, (NJ - 1) * pairs)], c_recv)


def body(
    amplitudes, amplitude_map, integrals, integral_map, pair_list, occupied_energy, virtual_energy
):
    pair_count, rows, cols = amplitudes.shape
    q = pair_count // NJ // CHUNKS
    hbm = pl.BlockSpec(memory_space=pl.ANY)
    dma = pltpu.SemaphoreType.DMA
    block = pltpu.VMEM((CHUNKS, NJ, q, rows, cols), jnp.bfloat16)
    return pl.pallas_call(
        kernel,
        out_shape=jax.ShapeDtypeStruct(amplitudes.shape, jnp.bfloat16),
        in_specs=[hbm] * 8,
        out_specs=pl.BlockSpec(memory_space=pl.ANY),
        scratch_shapes=[
            pltpu.SMEM(amplitude_map.shape, jnp.int32),
            pltpu.SMEM(integral_map.shape, jnp.int32),
            pltpu.SMEM((2, pair_count), jnp.int32),
            pltpu.SMEM(occupied_energy.shape, jnp.float32),
            pltpu.SMEM(virtual_energy.shape, jnp.float32),
            pltpu.VMEM((1, virtual_energy.size), jnp.float32),
            pltpu.VMEM((NJ, pair_count // NJ, rows, cols), jnp.bfloat16),
            block,
            block,
            pltpu.VMEM((CHUNKS + HEAD, NJ, q, rows, cols), jnp.bfloat16),
            block,
            pltpu.VMEM((NZL, TILE, 256), jnp.bfloat16),
            pltpu.VMEM((NY, NC, 2, 256, NZL * TILE), jnp.bfloat16),
            pltpu.VMEM((4, CHUNKS, q * rows, 256), jnp.float32),
            pltpu.VMEM((TILE, 128), jnp.float32),
            dma((CHUNKS,)),
            dma((CHUNKS,)),
            dma((CHUNKS,)),
            dma((CHUNKS,)),
            dma((CHUNKS,)),
            dma((CHUNKS,)),
            dma((CHUNKS,)),
            dma,
            dma((CHUNKS,)),
            dma((7,)),
            dma((7,)),
            dma((NX - 1,)),
            dma((2,)),
            dma((NY - 1,)),
            dma((NY,)),
            dma((NY,)),
            dma((NY,)),
            dma((9,)),
            dma((HEAD,)),
            dma((HEAD,)),
        ],
        compiler_params=pltpu.CompilerParams(
            collective_id=0, has_side_effects=True, vmem_limit_bytes=60 * 1024 * 1024
        ),
        cost_estimate=pl.CostEstimate(
            flops=2 * 1024 * 2048 * 1024, bytes_accessed=8 * 1024 * 1024, transcendentals=0
        ),
    )(
        amplitudes.reshape(NJ, pair_count // NJ, rows, cols),
        amplitude_map,
        integrals,
        integral_map,
        pair_list.T,
        occupied_energy,
        virtual_energy,
        virtual_energy.reshape(1, -1),
    )


def solution(mesh):
    in_specs = (
        P(None, "blk", "grp"),
        P("blk", "grp"),
        P("blk", None),
        P("blk", None),
        P(),
        P(),
        P(),
    )
    out_specs = P(None, "blk", "grp")
    return jax.shard_map(body, mesh=mesh, in_specs=in_specs, out_specs=out_specs, check_vma=False)
```

```python
import jax
import jax.numpy as jnp
from jax import lax
from jax.experimental import pallas as pl
from jax.experimental.pallas import tpu as pltpu
from jax.sharding import PartitionSpec as P

MESH = pl.DeviceIdType.MESH
TILE = 64
NX, NZ, NZL, NJ, NY, NC = 4, 16, 8, 8, 4, 2
CHUNKS = 16
HEAD, AHEAD = 2, 4
GROUP = 4
LEGS = (5, 3)


def drain(ref, sem):
    pltpu.make_async_copy(ref, ref, sem).wait()


def kernel(
    amp_hbm,
    amp_map_hbm,
    int_hbm,
    int_map_hbm,
    pair_hbm,
    occ_hbm,
    ve_hbm,
    ve_row_hbm,
    out_ref,
    amp_map_ref,
    int_map_ref,
    pair_ref,
    occ_ref,
    ve_smem,
    ve_row,
    masked,
    ybuf,
    relay,
    zbuf,
    cbuf,
    bline,
    bfull,
    own_acc,
    erow,
    y_send,
    y_recv,
    z_send,
    z_recv,
    f_send,
    f_recv,
    c_send,
    c_recv,
    own_sem,
    bz_send,
    bz_recv,
    bx_send,
    bx_recv,
    by_send,
    by_recv,
    bc_send,
    bc_recv,
    in_sem,
    hand_send,
    hand_recv,
):
    b = lax.axis_index("blk")
    g = lax.axis_index("grp")
    x, zl = b // NZL, b % NZL
    h, j = g // NJ, g % NJ
    y, c = j // NC, j % NC
    z = h * NZL + zl
    pairs = amp_hbm.shape[1]
    q = pairs // CHUNKS
    half_cols = NJ * 128

    def at_z(zz):
        zz = (zz + NZ) % NZ
        return (x * NZL + zz % NZL, (zz // NZL) * NJ + j)

    def at_j(jj):
        return (b, h * NJ + jj)

    def at_x(xx):
        return (xx * NZL + zl, g)

    peers = [at_z(z + d) for d in (1, -1, 3, -3, 5, -5)]
    peers += [at_j((j + d) % NJ) for d in range(1, NJ)]
    peers += [at_x((x + d) % NX) for d in range(1, NX)]
    barrier = pltpu.get_barrier_semaphore()
    for peer in peers:
        pl.semaphore_signal(barrier, inc=1, device_id=peer, device_id_type=MESH)

    first, rest = pl.ds(0, HEAD * q), pl.ds(HEAD * q, pairs - HEAD * q)
    loads = [
        pltpu.make_async_copy(src, dst, in_sem.at[i])
        for i, (src, dst) in enumerate(
            [
                (amp_map_hbm, amp_map_ref),
                (amp_hbm.at[:, first], masked.at[:, first]),
                (int_map_hbm, int_map_ref),
                (int_hbm.at[:, pl.ds(pl.multiple_of(j * 256, 128), 256)], bline.at[zl]),
                (amp_hbm.at[:, rest], masked.at[:, rest]),
                (pair_hbm, pair_ref),
                (occ_hbm, occ_ref),
                (ve_hbm, ve_smem),
                (ve_row_hbm, ve_row),
            ]
        )
    ]
    for load in loads:
        load.start()

    lane = lax.broadcasted_iota(jnp.int32, (1, 128), 1)

    def lane_mask(left, right):
        left, right = left.astype(jnp.float32), right.astype(jnp.float32)
        return jnp.where(lane < TILE, left, right).astype(jnp.bfloat16)

    loads[0].wait()
    amp_mask = lane_mask(amp_map_ref[0, 0], amp_map_ref[0, 1])

    def mask_chunk(k):
        for p in range(q):
            masked[:, k * q + p] = masked[:, k * q + p] * amp_mask[None]
            ybuf[k, j, p] = masked[j, k * q + p]

    loads[1].wait()
    for k in range(HEAD):
        mask_chunk(k)
    pl.semaphore_wait(barrier, len(peers))

    def send_chunk(k):
        for d in range(1, NJ):
            jj = (j + d) % NJ
            pltpu.make_async_remote_copy(
                src_ref=masked.at[jj, pl.ds(k * q, q)],
                dst_ref=ybuf.at[k, j],
                send_sem=y_send.at[k],
                recv_sem=y_recv.at[k],
                device_id=at_j(jj),
                device_id_type=MESH,
            ).start()

    def first_leg(k):
        return pltpu.make_async_remote_copy(
            src_ref=ybuf.at[k],
            dst_ref=relay.at[k],
            send_sem=z_send.at[k],
            recv_sem=z_recv.at[k],
            device_id=at_z(z + LEGS[0] * (1 - 2 * c)),
            device_id_type=MESH,
        )

    def second_leg(k, part):
        slot = (k + CHUNKS - HEAD) % CHUNKS + HEAD
        return pltpu.make_async_remote_copy(
            src_ref=relay.at[k, pl.ds(4 * part, 4)],
            dst_ref=zbuf.at[slot, pl.ds(4 * part, 4)],
            send_sem=f_send.at[k, part],
            recv_sem=f_recv.at[k, part],
            device_id=at_z(z + LEGS[1] * (1 - 2 * c)),
            device_id_type=MESH,
        )

    def head_leg(k):
        return pltpu.make_async_remote_copy(
            src_ref=masked.at[:, pl.ds(k * q, q)],
            dst_ref=relay.at[k],
            send_sem=z_send.at[k],
            recv_sem=z_recv.at[k],
            device_id=at_z(z + LEGS[0] * (1 - 2 * c)),
            device_id_type=MESH,
        )

    def hand_on(k):
        for d in range(1, NJ):
            jj = (j + d) % NJ
            pltpu.make_async_remote_copy(
                src_ref=zbuf.at[CHUNKS + k, jj],
                dst_ref=zbuf.at[k, j],
                send_sem=hand_send.at[k],
                recv_sem=hand_recv.at[k],
                device_id=at_j(jj),
                device_id_type=MESH,
            ).start()
        zbuf[k, j] = zbuf[CHUNKS + k, j]

    for k in range(HEAD):
        head_leg(k).start()
    loads[4].wait()
    mask_chunk(HEAD)
    send_chunk(HEAD)
    loads[2].wait()
    loads[3].wait()
    for half in range(2):
        tile = 4 * j + 2 * half
        cols = slice(half * 128, half * 128 + 128)
        int_mask = lane_mask(int_map_ref[0, tile], int_map_ref[0, tile + 1])
        bline[zl, :, cols] = bline[zl, :, cols] * int_mask

    def b_hop(r, way):
        step = 1 if way == 0 else -1
        slot = (z - step * (r - 1) + NZ) % NZL
        return pltpu.make_async_remote_copy(
            src_ref=bline.at[slot],
            dst_ref=bline.at[slot],
            send_sem=bz_send.at[4 * way + r - 1],
            recv_sem=bz_recv.at[4 * way + r - 1],
            device_id=at_z(z + step),
            device_id_type=MESH,
        )

    def b_arrived(r, way):
        step = 1 if way == 0 else -1
        drain(bline.at[(z - step * r + NZ) % NZL], bz_recv.at[4 * way + r - 1])

    for way in range(2):
        b_hop(1, way).start()
    for k in range(HEAD + 1, AHEAD):
        mask_chunk(k)
        send_chunk(k)

    in_half = x // 2 == h

    def b_along_x():
        b_arrived(4, 0)

        @pl.when(in_half)
        def _():
            bfull[y, c, x % 2] = bline[...].reshape(NZL * TILE, 256).T
            for d in range(1, NX):
                pltpu.make_async_remote_copy(
                    src_ref=bfull.at[y, c, x % 2],
                    dst_ref=bfull.at[y, c, x % 2],
                    send_sem=bx_send.at[d - 1],
                    recv_sem=bx_recv.at[x % 2],
                    device_id=at_x((x + d) % NX),
                    device_id_type=MESH,
                ).start()

    def b_along_y():
        for xx in range(2):

            @pl.when(x != 2 * h + xx)
            def _():
                drain(bfull.at[y, c, xx], bx_recv.at[xx])

        for d in range(1, NY):
            pltpu.make_async_remote_copy(
                src_ref=bfull.at[y, c],
                dst_ref=bfull.at[y, c],
                send_sem=by_send.at[d - 1],
                recv_sem=by_recv.at[y],
                device_id=at_j(((y + d) % NY) * NC + c),
                device_id_type=MESH,
            ).start()

    def b_core():
        for d in range(1, NY):
            yy = (y + d) % NY
            drain(bfull.at[yy, c], by_recv.at[yy])
        return b_core_copies()

    def b_core_copies():
        return [
            pltpu.make_async_remote_copy(
                src_ref=bfull.at[yy, c],
                dst_ref=bfull.at[yy, c],
                send_sem=bc_send.at[yy],
                recv_sem=bc_recv.at[yy],
                device_id=at_j(y * NC + 1 - c),
                device_id_type=MESH,
            )
            for yy in range(NY)
        ]

    def weights(hh, i, n):
        cols = pl.ds(pl.multiple_of((n % 2) * 256, 256), 256)
        return bfull[2 * hh + i // 2, i % 2, n // 2, :, cols]

    def rows_of(buf, first, count, i):
        blocks = [
            buf[pl.ds(first, count), 2 * i + e].reshape(count * q * TILE, 128) for e in range(2)
        ]
        return jnp.concatenate(blocks, axis=1)

    def own_half(group):
        @pl.loop(0, 4)
        def _(n):
            acc = jnp.zeros((GROUP * q * TILE, 256), jnp.float32)
            for i in range(4):
                acc += jnp.dot(
                    rows_of(ybuf, group * GROUP, GROUP, i),
                    weights(h, i, n),
                    preferred_element_type=jnp.float32,
                )
            own_acc[n, pl.ds(group * GROUP, GROUP)] = acc.reshape(GROUP, q * TILE, 256)

    def half_product(k):
        @pl.loop(0, 4)
        def _(n):
            acc = own_acc[n, k]
            for i in range(2):
                acc += jnp.dot(
                    rows_of(zbuf, k, 1, i),
                    weights(1 - h, i, n),
                    preferred_element_type=jnp.float32,
                )
            own_acc[n, k] = acc

    def compute(k):
        @pl.loop(0, 4)
        def _(step):
            n = (step + y) % 4
            acc = own_acc[n, k]
            for i in range(2, 4):
                acc += jnp.dot(
                    rows_of(zbuf, k, 1, i),
                    weights(1 - h, i, n),
                    preferred_element_type=jnp.float32,
                )
            ladder = acc.astype(jnp.bfloat16).astype(jnp.float32)
            for e in range(2):
                start = pl.multiple_of(h * half_cols + n * 256 + e * 128, 128)
                virt = erow[...] + ve_row[:, pl.ds(start, 128)]
                for p in range(q):
                    pair = j * pairs + k * q + p
                    shift = occ_ref[pair_ref[0, pair]] + occ_ref[pair_ref[1, pair]]
                    block = ladder[p * TILE : (p + 1) * TILE, e * 128 : (e + 1) * 128]
                    cbuf[k, 2 * n + e, p] = (block / (virt - shift)).astype(jnp.bfloat16)

            for e in range(2):
                jj = 2 * n + e

                @pl.when(jj != j)
                def _():
                    pltpu.make_async_remote_copy(
                        src_ref=cbuf.at[k, jj],
                        dst_ref=out_ref.at[pl.ds(j * pairs + k * q, q)],
                        send_sem=c_send.at[k],
                        recv_sem=c_recv,
                        device_id=at_j(jj),
                        device_id_type=MESH,
                    ).start()

        own_copy(k).start()

    def own_copy(k):
        return pltpu.make_async_copy(
            cbuf.at[k, j], out_ref.at[pl.ds(j * pairs + k * q, q)], own_sem.at[k]
        )

    def sent(k):
        for part in range(2):
            second_leg(k, part).wait_send()
        drain(cbuf.at[k, pl.ds(0, NJ - 1)], c_send.at[k])
        own_copy(k).wait()

    def b_sent():
        for way in range(2):
            for r in range(1, 5 - way):
                b_hop(r, way).wait_send()

        @pl.when(in_half)
        def _():
            for d in range(1, NX):
                drain(bfull.at[y, c, x % 2], bx_send.at[d - 1])

        for d in range(1, NY):
            drain(bfull.at[y, c], by_send.at[d - 1])
        for copy in b_core_copies():
            copy.wait_send()

    def finish(k):
        drain(ybuf.at[k, pl.ds(0, NJ - 1)], y_send.at[k])
        first_leg(k).wait_send()

        @pl.when(k > 0)
        def _():
            sent(k - 1)

        for part in range(2):

            @pl.when(k >= HEAD)
            def _():
                second_leg(k, part).wait_recv()

            if part == 0:
                half_product(k)
        compute(k)

    lag1, lag2, start = 4, 8, 12

    @pl.loop(0, CHUNKS + lag2)
    def _(t):
        @pl.when(jnp.logical_and(t >= HEAD, t < CHUNKS))
        def _():
            drain(ybuf.at[t, pl.ds(0, NJ - 1)], y_recv.at[t])
            first_leg(t).start()

        for e in range(2):
            ahead = AHEAD + 2 * t + e

            @pl.when(ahead < CHUNKS)
            def _():
                mask_chunk(ahead)
                send_chunk(ahead)

        @pl.when(jnp.logical_and(t >= lag1, t < CHUNKS + lag1))
        def _():
            k = t - lag1
            first_leg(k).wait_recv()
            for part in range(2):
                second_leg(k, part).start()

        @pl.when(t == 7)
        def _():
            for k in range(HEAD):
                send_chunk(k)

        for r in range(1, 4):

            @pl.when(t == lag1 + r - 1)
            def _():
                for way in range(2):
                    b_arrived(r, way)
                    if r + way < 4:
                        b_hop(r + 1, way).start()

        @pl.when(t == 7)
        def _():
            b_along_x()
            for load in loads[5:]:
                load.wait()

            @pl.loop(0, TILE)
            def _(r):
                erow[pl.ds(r, 1), :] = jnp.full((1, 128), ve_smem[b * TILE + r], jnp.float32)

        @pl.when(jnp.logical_and(t >= lag2, t < lag2 + HEAD))
        def _():
            for part in range(2):
                second_leg(t - lag2, part).wait_recv()
            hand_on(t - lag2)

        @pl.when(t == 9)
        def _():
            b_along_y()

        @pl.when(t == 11)
        def _():
            for copy in b_core():
                copy.start()

        @pl.when(t == start)
        def _():
            other = 1 - c
            for yy in range(NY):
                drain(bfull.at[yy, other], bc_recv.at[yy])
            b_sent()
            for k in range(HEAD):
                drain(ybuf.at[k, pl.ds(0, NJ - 1)], y_recv.at[k])
                drain(zbuf.at[k, pl.ds(0, NJ - 1)], hand_recv.at[k])
                drain(zbuf.at[k, pl.ds(0, NJ - 1)], hand_send.at[k])

        @pl.when(jnp.logical_and(t >= start, t < start + CHUNKS // GROUP))
        def _():
            own_half(t - start)

        @pl.when(jnp.logical_and(t >= start, t < 2 * start - lag2))
        def _():
            for e in range(2):
                finish(2 * (t - start) + e)

        @pl.when(t >= 2 * start - lag2)
        def _():
            finish(t - lag2)

    sent(CHUNKS - 1)
    drain(out_ref.at[pl.ds(0, (NJ - 1) * pairs)], c_recv)


def body(
    amplitudes, amplitude_map, integrals, integral_map, pair_list, occupied_energy, virtual_energy
):
    pair_count, rows, cols = amplitudes.shape
    q = pair_count // NJ // CHUNKS
    hbm = pl.BlockSpec(memory_space=pl.ANY)
    dma = pltpu.SemaphoreType.DMA
    block = pltpu.VMEM((CHUNKS, NJ, q, rows, cols), jnp.bfloat16)
    return pl.pallas_call(
        kernel,
        out_shape=jax.ShapeDtypeStruct(amplitudes.shape, jnp.bfloat16),
        in_specs=[hbm] * 8,
        out_specs=pl.BlockSpec(memory_space=pl.ANY),
        scratch_shapes=[
            pltpu.SMEM(amplitude_map.shape, jnp.int32),
            pltpu.SMEM(integral_map.shape, jnp.int32),
            pltpu.SMEM((2, pair_count), jnp.int32),
            pltpu.SMEM(occupied_energy.shape, jnp.float32),
            pltpu.SMEM(virtual_energy.shape, jnp.float32),
            pltpu.VMEM((1, virtual_energy.size), jnp.float32),
            pltpu.VMEM((NJ, pair_count // NJ, rows, cols), jnp.bfloat16),
            block,
            block,
            pltpu.VMEM((CHUNKS + HEAD, NJ, q, rows, cols), jnp.bfloat16),
            block,
            pltpu.VMEM((NZL, TILE, 256), jnp.bfloat16),
            pltpu.VMEM((NY, NC, 2, 256, NZL * TILE), jnp.bfloat16),
            pltpu.VMEM((4, CHUNKS, q * rows, 256), jnp.float32),
            pltpu.VMEM((TILE, 128), jnp.float32),
            dma((CHUNKS,)),
            dma((CHUNKS,)),
            dma((CHUNKS,)),
            dma((CHUNKS,)),
            dma((CHUNKS, 2)),
            dma((CHUNKS, 2)),
            dma((CHUNKS,)),
            dma,
            dma((CHUNKS,)),
            dma((7,)),
            dma((7,)),
            dma((NX - 1,)),
            dma((2,)),
            dma((NY - 1,)),
            dma((NY,)),
            dma((NY,)),
            dma((NY,)),
            dma((9,)),
            dma((HEAD,)),
            dma((HEAD,)),
        ],
        compiler_params=pltpu.CompilerParams(
            collective_id=0, has_side_effects=True, vmem_limit_bytes=60 * 1024 * 1024
        ),
        cost_estimate=pl.CostEstimate(
            flops=2 * 1024 * 2048 * 1024, bytes_accessed=8 * 1024 * 1024, transcendentals=0
        ),
    )(
        amplitudes.reshape(NJ, pair_count // NJ, rows, cols),
        amplitude_map,
        integrals,
        integral_map,
        pair_list.T,
        occupied_energy,
        virtual_energy,
        virtual_energy.reshape(1, -1),
    )


def solution(mesh):
    in_specs = (
        P(None, "blk", "grp"),
        P("blk", "grp"),
        P("blk", None),
        P("blk", None),
        P(),
        P(),
        P(),
    )
    out_specs = P(None, "blk", "grp")
    return jax.shard_map(body, mesh=mesh, in_specs=in_specs, out_specs=out_specs, check_vma=False)
```

```python
import jax
import jax.numpy as jnp
from jax import lax
from jax.experimental import pallas as pl
from jax.experimental.pallas import tpu as pltpu
from jax.sharding import PartitionSpec as P

MESH = pl.DeviceIdType.MESH
TILE = 64
NX, NZ, NZL, NJ, NY, NC = 4, 16, 8, 8, 4, 2
CHUNKS = 16
HEAD, AHEAD = 2, 4
GROUP = 4
LEGS = (5, 3)


def drain(ref, sem):
    pltpu.make_async_copy(ref, ref, sem).wait()


def kernel(
    amp_hbm,
    amp_map_hbm,
    int_hbm,
    int_map_hbm,
    pair_hbm,
    occ_hbm,
    ve_hbm,
    ve_row_hbm,
    out_ref,
    amp_map_ref,
    int_map_ref,
    pair_ref,
    occ_ref,
    ve_smem,
    ve_row,
    masked,
    ybuf,
    relay,
    zbuf,
    cbuf,
    bline,
    bfull,
    own_acc,
    erow,
    y_send,
    y_recv,
    z_send,
    z_recv,
    f_send,
    f_recv,
    c_send,
    c_recv,
    own_sem,
    bz_send,
    bz_recv,
    bx_send,
    bx_recv,
    by_send,
    by_recv,
    bc_send,
    bc_recv,
    in_sem,
    hand_send,
    hand_recv,
):
    b = lax.axis_index("blk")
    g = lax.axis_index("grp")
    x, zl = b // NZL, b % NZL
    h, j = g // NJ, g % NJ
    y, c = j // NC, j % NC
    z = h * NZL + zl
    pairs = amp_hbm.shape[1]
    q = pairs // CHUNKS
    half_cols = NJ * 128

    def at_z(zz):
        zz = (zz + NZ) % NZ
        return (x * NZL + zz % NZL, (zz // NZL) * NJ + j)

    def at_j(jj):
        return (b, h * NJ + jj)

    def at_x(xx):
        return (xx * NZL + zl, g)

    peers = [at_z(z + d) for d in (1, -1, 3, -3, 5, -5)]
    peers += [at_j((j + d) % NJ) for d in range(1, NJ)]
    peers += [at_x((x + d) % NX) for d in range(1, NX)]
    barrier = pltpu.get_barrier_semaphore()
    for peer in peers:
        pl.semaphore_signal(barrier, inc=1, device_id=peer, device_id_type=MESH)

    first, rest = pl.ds(0, HEAD * q), pl.ds(HEAD * q, pairs - HEAD * q)
    loads = [
        pltpu.make_async_copy(src, dst, in_sem.at[i])
        for i, (src, dst) in enumerate(
            [
                (amp_map_hbm, amp_map_ref),
                (amp_hbm.at[:, first], masked.at[:, first]),
                (int_map_hbm, int_map_ref),
                (int_hbm.at[:, pl.ds(pl.multiple_of(j * 256, 128), 256)], bline.at[zl]),
                (amp_hbm.at[:, rest], masked.at[:, rest]),
                (pair_hbm, pair_ref),
                (occ_hbm, occ_ref),
                (ve_hbm, ve_smem),
                (ve_row_hbm, ve_row),
            ]
        )
    ]
    for load in loads:
        load.start()

    lane = lax.broadcasted_iota(jnp.int32, (1, 128), 1)

    def lane_mask(left, right):
        left, right = left.astype(jnp.float32), right.astype(jnp.float32)
        return jnp.where(lane < TILE, left, right).astype(jnp.bfloat16)

    loads[0].wait()
    amp_mask = lane_mask(amp_map_ref[0, 0], amp_map_ref[0, 1])

    def mask_chunk(k):
        for p in range(q):
            masked[:, k * q + p] = masked[:, k * q + p] * amp_mask[None]
            ybuf[k, j, p] = masked[j, k * q + p]

    loads[1].wait()
    for k in range(HEAD):
        mask_chunk(k)
    pl.semaphore_wait(barrier, len(peers))

    def send_chunk(k):
        for d in range(1, NJ):
            jj = (j + d) % NJ
            pltpu.make_async_remote_copy(
                src_ref=masked.at[jj, pl.ds(k * q, q)],
                dst_ref=ybuf.at[k, j],
                send_sem=y_send.at[k],
                recv_sem=y_recv.at[k],
                device_id=at_j(jj),
                device_id_type=MESH,
            ).start()

    def legs(k, first):
        slot = (k + CHUNKS - HEAD) % CHUNKS + HEAD
        src, dst = (ybuf, relay) if first else (relay, zbuf)
        hops = LEGS[0] if first else LEGS[1]
        ssem, rsem = (z_send, z_recv) if first else (f_send, f_recv)
        return [
            pltpu.make_async_remote_copy(
                src_ref=src.at[k],
                dst_ref=dst.at[k if first else slot],
                send_sem=ssem.at[k],
                recv_sem=rsem.at[k],
                device_id=at_z(z + hops * (1 - 2 * c)),
                device_id_type=MESH,
            )
        ]

    def head_leg(k):
        return pltpu.make_async_remote_copy(
            src_ref=masked.at[:, pl.ds(k * q, q)],
            dst_ref=relay.at[k],
            send_sem=z_send.at[k],
            recv_sem=z_recv.at[k],
            device_id=at_z(z + LEGS[0] * (1 - 2 * c)),
            device_id_type=MESH,
        )

    def hand_on(k):
        for d in range(1, NJ):
            jj = (j + d) % NJ
            pltpu.make_async_remote_copy(
                src_ref=zbuf.at[CHUNKS + k, jj],
                dst_ref=zbuf.at[k, j],
                send_sem=hand_send.at[k],
                recv_sem=hand_recv.at[k],
                device_id=at_j(jj),
                device_id_type=MESH,
            ).start()
        zbuf[k, j] = zbuf[CHUNKS + k, j]

    for k in range(HEAD):
        head_leg(k).start()
    loads[4].wait()
    mask_chunk(HEAD)
    send_chunk(HEAD)
    loads[2].wait()
    loads[3].wait()
    for half in range(2):
        tile = 4 * j + 2 * half
        cols = slice(half * 128, half * 128 + 128)
        int_mask = lane_mask(int_map_ref[0, tile], int_map_ref[0, tile + 1])
        bline[zl, :, cols] = bline[zl, :, cols] * int_mask

    def b_hop(r, way):
        step = 1 if way == 0 else -1
        slot = (z - step * (r - 1) + NZ) % NZL
        return pltpu.make_async_remote_copy(
            src_ref=bline.at[slot],
            dst_ref=bline.at[slot],
            send_sem=bz_send.at[4 * way + r - 1],
            recv_sem=bz_recv.at[4 * way + r - 1],
            device_id=at_z(z + step),
            device_id_type=MESH,
        )

    def b_arrived(r, way):
        step = 1 if way == 0 else -1
        drain(bline.at[(z - step * r + NZ) % NZL], bz_recv.at[4 * way + r - 1])

    for way in range(2):
        b_hop(1, way).start()
    for k in range(HEAD + 1, AHEAD):
        mask_chunk(k)
        send_chunk(k)

    in_half = x // 2 == h

    def b_along_x():
        b_arrived(4, 0)

        @pl.when(in_half)
        def _():
            bfull[y, c, x % 2] = bline[...].reshape(NZL * TILE, 256).T
            for d in range(1, NX):
                pltpu.make_async_remote_copy(
                    src_ref=bfull.at[y, c, x % 2],
                    dst_ref=bfull.at[y, c, x % 2],
                    send_sem=bx_send.at[d - 1],
                    recv_sem=bx_recv.at[x % 2],
                    device_id=at_x((x + d) % NX),
                    device_id_type=MESH,
                ).start()

    def b_along_y():
        for xx in range(2):

            @pl.when(x != 2 * h + xx)
            def _():
                drain(bfull.at[y, c, xx], bx_recv.at[xx])

        for d in range(1, NY):
            pltpu.make_async_remote_copy(
                src_ref=bfull.at[y, c],
                dst_ref=bfull.at[y, c],
                send_sem=by_send.at[d - 1],
                recv_sem=by_recv.at[y],
                device_id=at_j(((y + d) % NY) * NC + c),
                device_id_type=MESH,
            ).start()

    def b_core():
        for d in range(1, NY):
            yy = (y + d) % NY
            drain(bfull.at[yy, c], by_recv.at[yy])
        return b_core_copies()

    def b_core_copies():
        return [
            pltpu.make_async_remote_copy(
                src_ref=bfull.at[yy, c],
                dst_ref=bfull.at[yy, c],
                send_sem=bc_send.at[yy],
                recv_sem=bc_recv.at[yy],
                device_id=at_j(y * NC + 1 - c),
                device_id_type=MESH,
            )
            for yy in range(NY)
        ]

    def weights(hh, i, n):
        cols = pl.ds(pl.multiple_of((n % 2) * 256, 256), 256)
        return bfull[2 * hh + i // 2, i % 2, n // 2, :, cols]

    def rows_of(buf, first, count, i):
        blocks = [
            buf[pl.ds(first, count), 2 * i + e].reshape(count * q * TILE, 128) for e in range(2)
        ]
        return jnp.concatenate(blocks, axis=1)

    def own_half(group):
        @pl.loop(0, 4)
        def _(n):
            acc = jnp.zeros((GROUP * q * TILE, 256), jnp.float32)
            for i in range(4):
                acc += jnp.dot(
                    rows_of(ybuf, group * GROUP, GROUP, i),
                    weights(h, i, n),
                    preferred_element_type=jnp.float32,
                )
            own_acc[n, pl.ds(group * GROUP, GROUP)] = acc.reshape(GROUP, q * TILE, 256)

    def compute(k):
        @pl.loop(0, 4)
        def _(step):
            n = (step + y) % 4
            acc = own_acc[n, k]
            for i in range(4):
                acc += jnp.dot(
                    rows_of(zbuf, k, 1, i),
                    weights(1 - h, i, n),
                    preferred_element_type=jnp.float32,
                )
            ladder = acc.astype(jnp.bfloat16).astype(jnp.float32)
            for e in range(2):
                start = pl.multiple_of(h * half_cols + n * 256 + e * 128, 128)
                virt = erow[...] + ve_row[:, pl.ds(start, 128)]
                for p in range(q):
                    pair = j * pairs + k * q + p
                    shift = occ_ref[pair_ref[0, pair]] + occ_ref[pair_ref[1, pair]]
                    block = ladder[p * TILE : (p + 1) * TILE, e * 128 : (e + 1) * 128]
                    cbuf[k, 2 * n + e, p] = (block / (virt - shift)).astype(jnp.bfloat16)

            for e in range(2):
                jj = 2 * n + e

                @pl.when(jj != j)
                def _():
                    pltpu.make_async_remote_copy(
                        src_ref=cbuf.at[k, jj],
                        dst_ref=out_ref.at[pl.ds(j * pairs + k * q, q)],
                        send_sem=c_send.at[k],
                        recv_sem=c_recv,
                        device_id=at_j(jj),
                        device_id_type=MESH,
                    ).start()

        own_copy(k).start()

    def own_copy(k):
        return pltpu.make_async_copy(
            cbuf.at[k, j], out_ref.at[pl.ds(j * pairs + k * q, q)], own_sem.at[k]
        )

    def sent(k):
        for copy in legs(k, False):
            copy.wait_send()
        drain(cbuf.at[k, pl.ds(0, NJ - 1)], c_send.at[k])
        own_copy(k).wait()

    def b_sent():
        for way in range(2):
            for r in range(1, 5 - way):
                b_hop(r, way).wait_send()

        @pl.when(in_half)
        def _():
            for d in range(1, NX):
                drain(bfull.at[y, c, x % 2], bx_send.at[d - 1])

        for d in range(1, NY):
            drain(bfull.at[y, c], by_send.at[d - 1])
        for copy in b_core_copies():
            copy.wait_send()

    def finish(k):
        drain(ybuf.at[k, pl.ds(0, NJ - 1)], y_send.at[k])
        for copy in legs(k, True):
            copy.wait_send()

        @pl.when(k > 0)
        def _():
            sent(k - 1)

        @pl.when(k >= HEAD)
        def _():
            for copy in legs(k, False):
                copy.wait_recv()

        compute(k)

    lag1, lag2, start = 4, 8, 12

    @pl.loop(0, CHUNKS + lag2)
    def _(t):
        @pl.when(jnp.logical_and(t >= HEAD, t < CHUNKS))
        def _():
            drain(ybuf.at[t, pl.ds(0, NJ - 1)], y_recv.at[t])
            for copy in legs(t, True):
                copy.start()

        for e in range(2):
            ahead = AHEAD + 2 * t + e

            @pl.when(ahead < CHUNKS)
            def _():
                mask_chunk(ahead)
                send_chunk(ahead)

        @pl.when(jnp.logical_and(t >= lag1, t < CHUNKS + lag1))
        def _():
            k = t - lag1
            for first, second in zip(legs(k, True), legs(k, False)):
                first.wait_recv()
                second.start()

        @pl.when(t == 7)
        def _():
            for k in range(HEAD):
                send_chunk(k)

        for r in range(1, 4):

            @pl.when(t == lag1 + r - 1)
            def _():
                for way in range(2):
                    b_arrived(r, way)
                    if r + way < 4:
                        b_hop(r + 1, way).start()

        @pl.when(t == 7)
        def _():
            b_along_x()
            for load in loads[5:]:
                load.wait()

            @pl.loop(0, TILE)
            def _(r):
                erow[pl.ds(r, 1), :] = jnp.full((1, 128), ve_smem[b * TILE + r], jnp.float32)

        @pl.when(jnp.logical_and(t >= lag2, t < lag2 + HEAD))
        def _():
            for copy in legs(t - lag2, False):
                copy.wait_recv()
            hand_on(t - lag2)

        @pl.when(t == 9)
        def _():
            b_along_y()

        @pl.when(t == 11)
        def _():
            for copy in b_core():
                copy.start()

        @pl.when(t == start)
        def _():
            other = 1 - c
            for yy in range(NY):
                drain(bfull.at[yy, other], bc_recv.at[yy])
            b_sent()
            for k in range(HEAD):
                drain(ybuf.at[k, pl.ds(0, NJ - 1)], y_recv.at[k])
                drain(zbuf.at[k, pl.ds(0, NJ - 1)], hand_recv.at[k])
                drain(zbuf.at[k, pl.ds(0, NJ - 1)], hand_send.at[k])

        @pl.when(jnp.logical_and(t >= start, t < start + CHUNKS // GROUP))
        def _():
            own_half(t - start)

        @pl.when(jnp.logical_and(t >= start, t < 2 * start - lag2))
        def _():
            for e in range(2):
                finish(2 * (t - start) + e)

        @pl.when(t >= 2 * start - lag2)
        def _():
            finish(t - lag2)

    sent(CHUNKS - 1)
    drain(out_ref.at[pl.ds(0, (NJ - 1) * pairs)], c_recv)


def copy_out(src_ref, dst_ref, held, in_sems, out_sems):
    parts = in_sems.shape[0]
    size = held.shape[0] // parts
    slices = [pl.ds(i * size, size) for i in range(parts)]
    loads = [
        pltpu.make_async_copy(src_ref.at[part], held.at[part], in_sems.at[i])
        for i, part in enumerate(slices)
    ]
    stores = [
        pltpu.make_async_copy(held.at[part], dst_ref.at[part], out_sems.at[i])
        for i, part in enumerate(slices)
    ]
    for load in loads:
        load.start()
    for load, store in zip(loads, stores):
        load.wait()
        store.start()
    for store in stores:
        store.wait()


def body(
    amplitudes, amplitude_map, integrals, integral_map, pair_list, occupied_energy, virtual_energy
):
    pair_count, rows, cols = amplitudes.shape
    q = pair_count // NJ // CHUNKS
    hbm = pl.BlockSpec(memory_space=pl.ANY)
    dma = pltpu.SemaphoreType.DMA
    block = pltpu.VMEM((CHUNKS, NJ, q, rows, cols), jnp.bfloat16)
    update = pl.pallas_call(
        kernel,
        out_shape=jax.ShapeDtypeStruct(amplitudes.shape, jnp.bfloat16),
        in_specs=[hbm] * 8,
        out_specs=pl.BlockSpec(memory_space=pl.ANY),
        scratch_shapes=[
            pltpu.SMEM(amplitude_map.shape, jnp.int32),
            pltpu.SMEM(integral_map.shape, jnp.int32),
            pltpu.SMEM((2, pair_count), jnp.int32),
            pltpu.SMEM(occupied_energy.shape, jnp.float32),
            pltpu.SMEM(virtual_energy.shape, jnp.float32),
            pltpu.VMEM((1, virtual_energy.size), jnp.float32),
            pltpu.VMEM((NJ, pair_count // NJ, rows, cols), jnp.bfloat16),
            block,
            block,
            pltpu.VMEM((CHUNKS + HEAD, NJ, q, rows, cols), jnp.bfloat16),
            block,
            pltpu.VMEM((NZL, TILE, 256), jnp.bfloat16),
            pltpu.VMEM((NY, NC, 2, 256, NZL * TILE), jnp.bfloat16),
            pltpu.VMEM((4, CHUNKS, q * rows, 256), jnp.float32),
            pltpu.VMEM((TILE, 128), jnp.float32),
            dma((CHUNKS,)),
            dma((CHUNKS,)),
            dma((CHUNKS,)),
            dma((CHUNKS,)),
            dma((CHUNKS,)),
            dma((CHUNKS,)),
            dma((CHUNKS,)),
            dma,
            dma((CHUNKS,)),
            dma((7,)),
            dma((7,)),
            dma((NX - 1,)),
            dma((2,)),
            dma((NY - 1,)),
            dma((NY,)),
            dma((NY,)),
            dma((NY,)),
            dma((9,)),
            dma((HEAD,)),
            dma((HEAD,)),
        ],
        compiler_params=pltpu.CompilerParams(
            collective_id=0, has_side_effects=True, vmem_limit_bytes=60 * 1024 * 1024
        ),
        cost_estimate=pl.CostEstimate(
            flops=2 * 1024 * 2048 * 1024, bytes_accessed=8 * 1024 * 1024, transcendentals=0
        ),
    )(
        amplitudes.reshape(NJ, pair_count // NJ, rows, cols),
        amplitude_map,
        integrals,
        integral_map,
        pair_list.T,
        occupied_energy,
        virtual_energy,
        virtual_energy.reshape(1, -1),
    )
    return pl.pallas_call(
        copy_out,
        out_shape=jax.ShapeDtypeStruct(amplitudes.shape, jnp.bfloat16),
        in_specs=[hbm],
        out_specs=hbm,
        scratch_shapes=[pltpu.VMEM(amplitudes.shape, jnp.bfloat16), dma((8,)), dma((8,))],
        compiler_params=pltpu.CompilerParams(vmem_limit_bytes=60 * 1024 * 1024),
    )(update)


def solution(mesh):
    in_specs = (
        P(None, "blk", "grp"),
        P("blk", "grp"),
        P("blk", None),
        P("blk", None),
        P(),
        P(),
        P(),
    )
    out_specs = P(None, "blk", "grp")
    return jax.shard_map(body, mesh=mesh, in_specs=in_specs, out_specs=out_specs, check_vma=False)
```

```python
import jax
import jax.numpy as jnp
from jax import lax
from jax.experimental import pallas as pl
from jax.experimental.pallas import tpu as pltpu
from jax.sharding import PartitionSpec as P

MESH = pl.DeviceIdType.MESH
TILE = 64
NX, NZ, NZL, NJ, NY, NC = 4, 16, 8, 8, 4, 2
CHUNKS = 16
HEAD, AHEAD = 4, 6
GROUP = 4
LEGS = (5, 3)


def drain(ref, sem):
    pltpu.make_async_copy(ref, ref, sem).wait()


def kernel(
    amp_hbm,
    amp_map_hbm,
    int_hbm,
    int_map_hbm,
    pair_hbm,
    occ_hbm,
    ve_hbm,
    ve_row_hbm,
    out_ref,
    amp_map_ref,
    int_map_ref,
    pair_ref,
    occ_ref,
    ve_smem,
    ve_row,
    masked,
    ybuf,
    relay,
    zbuf,
    cbuf,
    bline,
    bfull,
    own_acc,
    erow,
    y_send,
    y_recv,
    z_send,
    z_recv,
    f_send,
    f_recv,
    c_send,
    c_recv,
    own_sem,
    bz_send,
    bz_recv,
    bx_send,
    bx_recv,
    by_send,
    by_recv,
    bc_send,
    bc_recv,
    in_sem,
    hand_send,
    hand_recv,
):
    b = lax.axis_index("blk")
    g = lax.axis_index("grp")
    x, zl = b // NZL, b % NZL
    h, j = g // NJ, g % NJ
    y, c = j // NC, j % NC
    z = h * NZL + zl
    pairs = amp_hbm.shape[1]
    q = pairs // CHUNKS
    half_cols = NJ * 128

    def at_z(zz):
        zz = (zz + NZ) % NZ
        return (x * NZL + zz % NZL, (zz // NZL) * NJ + j)

    def at_j(jj):
        return (b, h * NJ + jj)

    def at_x(xx):
        return (xx * NZL + zl, g)

    peers = [at_z(z + d) for d in (1, -1, 3, -3, 5, -5)]
    peers += [at_j((j + d) % NJ) for d in range(1, NJ)]
    peers += [at_x((x + d) % NX) for d in range(1, NX)]
    barrier = pltpu.get_barrier_semaphore()
    for peer in peers:
        pl.semaphore_signal(barrier, inc=1, device_id=peer, device_id_type=MESH)

    first, rest = pl.ds(0, HEAD * q), pl.ds(HEAD * q, pairs - HEAD * q)
    loads = [
        pltpu.make_async_copy(src, dst, in_sem.at[i])
        for i, (src, dst) in enumerate(
            [
                (amp_map_hbm, amp_map_ref),
                (amp_hbm.at[:, first], masked.at[:, first]),
                (int_map_hbm, int_map_ref),
                (int_hbm.at[:, pl.ds(pl.multiple_of(j * 256, 128), 256)], bline.at[zl]),
                (amp_hbm.at[:, rest], masked.at[:, rest]),
                (pair_hbm, pair_ref),
                (occ_hbm, occ_ref),
                (ve_hbm, ve_smem),
                (ve_row_hbm, ve_row),
            ]
        )
    ]
    for load in loads:
        load.start()

    lane = lax.broadcasted_iota(jnp.int32, (1, 128), 1)

    def lane_mask(left, right):
        left, right = left.astype(jnp.float32), right.astype(jnp.float32)
        return jnp.where(lane < TILE, left, right).astype(jnp.bfloat16)

    loads[0].wait()
    amp_mask = lane_mask(amp_map_ref[0, 0], amp_map_ref[0, 1])

    def mask_chunk(k):
        for p in range(q):
            masked[:, k * q + p] = masked[:, k * q + p] * amp_mask[None]
            ybuf[k, j, p] = masked[j, k * q + p]

    loads[1].wait()
    for k in range(HEAD):
        mask_chunk(k)
    pl.semaphore_wait(barrier, len(peers))

    def send_chunk(k):
        for d in range(1, NJ):
            jj = (j + d) % NJ
            pltpu.make_async_remote_copy(
                src_ref=masked.at[jj, pl.ds(k * q, q)],
                dst_ref=ybuf.at[k, j],
                send_sem=y_send.at[k],
                recv_sem=y_recv.at[k],
                device_id=at_j(jj),
                device_id_type=MESH,
            ).start()

    def legs(k, first):
        slot = (k + CHUNKS - HEAD) % CHUNKS + HEAD
        src, dst = (ybuf, relay) if first else (relay, zbuf)
        hops = LEGS[0] if first else LEGS[1]
        ssem, rsem = (z_send, z_recv) if first else (f_send, f_recv)
        return [
            pltpu.make_async_remote_copy(
                src_ref=src.at[k],
                dst_ref=dst.at[k if first else slot],
                send_sem=ssem.at[k],
                recv_sem=rsem.at[k],
                device_id=at_z(z + hops * (1 - 2 * c)),
                device_id_type=MESH,
            )
        ]

    def head_leg(k):
        return pltpu.make_async_remote_copy(
            src_ref=masked.at[:, pl.ds(k * q, q)],
            dst_ref=relay.at[k],
            send_sem=z_send.at[k],
            recv_sem=z_recv.at[k],
            device_id=at_z(z + LEGS[0] * (1 - 2 * c)),
            device_id_type=MESH,
        )

    def hand_on(k):
        for d in range(1, NJ):
            jj = (j + d) % NJ
            pltpu.make_async_remote_copy(
                src_ref=zbuf.at[CHUNKS + k, jj],
                dst_ref=zbuf.at[k, j],
                send_sem=hand_send.at[k],
                recv_sem=hand_recv.at[k],
                device_id=at_j(jj),
                device_id_type=MESH,
            ).start()
        zbuf[k, j] = zbuf[CHUNKS + k, j]

    for k in range(HEAD):
        head_leg(k).start()
    loads[4].wait()
    mask_chunk(HEAD)
    send_chunk(HEAD)
    loads[2].wait()
    loads[3].wait()
    for half in range(2):
        tile = 4 * j + 2 * half
        cols = slice(half * 128, half * 128 + 128)
        int_mask = lane_mask(int_map_ref[0, tile], int_map_ref[0, tile + 1])
        bline[zl, :, cols] = bline[zl, :, cols] * int_mask

    def b_hop(r, way):
        step = 1 if way == 0 else -1
        slot = (z - step * (r - 1) + NZ) % NZL
        return pltpu.make_async_remote_copy(
            src_ref=bline.at[slot],
            dst_ref=bline.at[slot],
            send_sem=bz_send.at[4 * way + r - 1],
            recv_sem=bz_recv.at[4 * way + r - 1],
            device_id=at_z(z + step),
            device_id_type=MESH,
        )

    def b_arrived(r, way):
        step = 1 if way == 0 else -1
        drain(bline.at[(z - step * r + NZ) % NZL], bz_recv.at[4 * way + r - 1])

    for way in range(2):
        b_hop(1, way).start()
    for k in range(HEAD + 1, AHEAD):
        mask_chunk(k)
        send_chunk(k)

    in_half = x // 2 == h

    def b_along_x():
        b_arrived(4, 0)

        @pl.when(in_half)
        def _():
            bfull[y, c, x % 2] = bline[...].reshape(NZL * TILE, 256).T
            for d in range(1, NX):
                pltpu.make_async_remote_copy(
                    src_ref=bfull.at[y, c, x % 2],
                    dst_ref=bfull.at[y, c, x % 2],
                    send_sem=bx_send.at[d - 1],
                    recv_sem=bx_recv.at[x % 2],
                    device_id=at_x((x + d) % NX),
                    device_id_type=MESH,
                ).start()

    def b_along_y():
        for xx in range(2):

            @pl.when(x != 2 * h + xx)
            def _():
                drain(bfull.at[y, c, xx], bx_recv.at[xx])

        for d in range(1, NY):
            pltpu.make_async_remote_copy(
                src_ref=bfull.at[y, c],
                dst_ref=bfull.at[y, c],
                send_sem=by_send.at[d - 1],
                recv_sem=by_recv.at[y],
                device_id=at_j(((y + d) % NY) * NC + c),
                device_id_type=MESH,
            ).start()

    def b_core():
        for d in range(1, NY):
            yy = (y + d) % NY
            drain(bfull.at[yy, c], by_recv.at[yy])
        return b_core_copies()

    def b_core_copies():
        return [
            pltpu.make_async_remote_copy(
                src_ref=bfull.at[yy, c],
                dst_ref=bfull.at[yy, c],
                send_sem=bc_send.at[yy],
                recv_sem=bc_recv.at[yy],
                device_id=at_j(y * NC + 1 - c),
                device_id_type=MESH,
            )
            for yy in range(NY)
        ]

    def weights(hh, i, n):
        cols = pl.ds(pl.multiple_of((n % 2) * 256, 256), 256)
        return bfull[2 * hh + i // 2, i % 2, n // 2, :, cols]

    def rows_of(buf, first, count, i):
        blocks = [
            buf[pl.ds(first, count), 2 * i + e].reshape(count * q * TILE, 128) for e in range(2)
        ]
        return jnp.concatenate(blocks, axis=1)

    def own_half(group):
        @pl.loop(0, 4)
        def _(n):
            acc = jnp.zeros((GROUP * q * TILE, 256), jnp.float32)
            for i in range(4):
                acc += jnp.dot(
                    rows_of(ybuf, group * GROUP, GROUP, i),
                    weights(h, i, n),
                    preferred_element_type=jnp.float32,
                )
            own_acc[n, pl.ds(group * GROUP, GROUP)] = acc.reshape(GROUP, q * TILE, 256)

    def compute(k):
        @pl.loop(0, 4)
        def _(step):
            n = (step + y) % 4
            acc = own_acc[n, k]
            for i in range(4):
                acc += jnp.dot(
                    rows_of(zbuf, k, 1, i),
                    weights(1 - h, i, n),
                    preferred_element_type=jnp.float32,
                )
            ladder = acc.astype(jnp.bfloat16).astype(jnp.float32)
            for e in range(2):
                start = pl.multiple_of(h * half_cols + n * 256 + e * 128, 128)
                virt = erow[...] + ve_row[:, pl.ds(start, 128)]
                for p in range(q):
                    pair = j * pairs + k * q + p
                    shift = occ_ref[pair_ref[0, pair]] + occ_ref[pair_ref[1, pair]]
                    block = ladder[p * TILE : (p + 1) * TILE, e * 128 : (e + 1) * 128]
                    cbuf[k, 2 * n + e, p] = (block / (virt - shift)).astype(jnp.bfloat16)

            for e in range(2):
                jj = 2 * n + e

                @pl.when(jj != j)
                def _():
                    pltpu.make_async_remote_copy(
                        src_ref=cbuf.at[k, jj],
                        dst_ref=out_ref.at[pl.ds(j * pairs + k * q, q)],
                        send_sem=c_send.at[k],
                        recv_sem=c_recv,
                        device_id=at_j(jj),
                        device_id_type=MESH,
                    ).start()

        own_copy(k).start()

    def own_copy(k):
        return pltpu.make_async_copy(
            cbuf.at[k, j], out_ref.at[pl.ds(j * pairs + k * q, q)], own_sem.at[k]
        )

    def sent(k):
        for copy in legs(k, False):
            copy.wait_send()
        drain(cbuf.at[k, pl.ds(0, NJ - 1)], c_send.at[k])
        own_copy(k).wait()

    def b_sent():
        for way in range(2):
            for r in range(1, 5 - way):
                b_hop(r, way).wait_send()

        @pl.when(in_half)
        def _():
            for d in range(1, NX):
                drain(bfull.at[y, c, x % 2], bx_send.at[d - 1])

        for d in range(1, NY):
            drain(bfull.at[y, c], by_send.at[d - 1])
        for copy in b_core_copies():
            copy.wait_send()

    def finish(k):
        drain(ybuf.at[k, pl.ds(0, NJ - 1)], y_send.at[k])
        for copy in legs(k, True):
            copy.wait_send()

        @pl.when(k > 0)
        def _():
            sent(k - 1)

        @pl.when(k >= HEAD)
        def _():
            for copy in legs(k, False):
                copy.wait_recv()

        compute(k)

    lag1, lag2, start = 4, 8, 12

    @pl.loop(0, CHUNKS + lag2)
    def _(t):
        @pl.when(jnp.logical_and(t >= HEAD, t < CHUNKS))
        def _():
            drain(ybuf.at[t, pl.ds(0, NJ - 1)], y_recv.at[t])
            for copy in legs(t, True):
                copy.start()

        for e in range(2):
            ahead = AHEAD + 2 * t + e

            @pl.when(ahead < CHUNKS)
            def _():
                mask_chunk(ahead)
                send_chunk(ahead)

        @pl.when(jnp.logical_and(t >= lag1, t < CHUNKS + lag1))
        def _():
            k = t - lag1
            for first, second in zip(legs(k, True), legs(k, False)):
                first.wait_recv()
                second.start()

        @pl.when(t == 7)
        def _():
            for k in range(HEAD):
                send_chunk(k)

        for r in range(1, 4):

            @pl.when(t == lag1 + r - 1)
            def _():
                for way in range(2):
                    b_arrived(r, way)
                    if r + way < 4:
                        b_hop(r + 1, way).start()

        @pl.when(t == 7)
        def _():
            b_along_x()
            for load in loads[5:]:
                load.wait()

            @pl.loop(0, TILE)
            def _(r):
                erow[pl.ds(r, 1), :] = jnp.full((1, 128), ve_smem[b * TILE + r], jnp.float32)

        @pl.when(jnp.logical_and(t >= lag2, t < lag2 + HEAD))
        def _():
            for copy in legs(t - lag2, False):
                copy.wait_recv()
            hand_on(t - lag2)

        @pl.when(t == 9)
        def _():
            b_along_y()

        @pl.when(t == 11)
        def _():
            for copy in b_core():
                copy.start()

        @pl.when(t == start)
        def _():
            other = 1 - c
            for yy in range(NY):
                drain(bfull.at[yy, other], bc_recv.at[yy])
            b_sent()
            for k in range(HEAD):
                drain(ybuf.at[k, pl.ds(0, NJ - 1)], y_recv.at[k])
                drain(zbuf.at[k, pl.ds(0, NJ - 1)], hand_recv.at[k])
                drain(zbuf.at[k, pl.ds(0, NJ - 1)], hand_send.at[k])

        @pl.when(jnp.logical_and(t >= start, t < start + CHUNKS // GROUP))
        def _():
            own_half(t - start)

        @pl.when(jnp.logical_and(t >= start, t < 2 * start - lag2))
        def _():
            for e in range(2):
                finish(2 * (t - start) + e)

        @pl.when(t >= 2 * start - lag2)
        def _():
            finish(t - lag2)

    sent(CHUNKS - 1)
    drain(out_ref.at[pl.ds(0, (NJ - 1) * pairs)], c_recv)


def copy_out(src_ref, dst_ref, held, in_sems, out_sems):
    parts = in_sems.shape[0]
    size = held.shape[0] // parts
    slices = [pl.ds(i * size, size) for i in range(parts)]
    loads = [
        pltpu.make_async_copy(src_ref.at[part], held.at[part], in_sems.at[i])
        for i, part in enumerate(slices)
    ]
    stores = [
        pltpu.make_async_copy(held.at[part], dst_ref.at[part], out_sems.at[i])
        for i, part in enumerate(slices)
    ]
    for load in loads:
        load.start()
    for load, store in zip(loads, stores):
        load.wait()
        store.start()
    for store in stores:
        store.wait()


def body(
    amplitudes, amplitude_map, integrals, integral_map, pair_list, occupied_energy, virtual_energy
):
    pair_count, rows, cols = amplitudes.shape
    q = pair_count // NJ // CHUNKS
    hbm = pl.BlockSpec(memory_space=pl.ANY)
    dma = pltpu.SemaphoreType.DMA
    block = pltpu.VMEM((CHUNKS, NJ, q, rows, cols), jnp.bfloat16)
    update = pl.pallas_call(
        kernel,
        out_shape=jax.ShapeDtypeStruct(amplitudes.shape, jnp.bfloat16),
        in_specs=[hbm] * 8,
        out_specs=pl.BlockSpec(memory_space=pl.ANY),
        scratch_shapes=[
            pltpu.SMEM(amplitude_map.shape, jnp.int32),
            pltpu.SMEM(integral_map.shape, jnp.int32),
            pltpu.SMEM((2, pair_count), jnp.int32),
            pltpu.SMEM(occupied_energy.shape, jnp.float32),
            pltpu.SMEM(virtual_energy.shape, jnp.float32),
            pltpu.VMEM((1, virtual_energy.size), jnp.float32),
            pltpu.VMEM((NJ, pair_count // NJ, rows, cols), jnp.bfloat16),
            block,
            block,
            pltpu.VMEM((CHUNKS + HEAD, NJ, q, rows, cols), jnp.bfloat16),
            block,
            pltpu.VMEM((NZL, TILE, 256), jnp.bfloat16),
            pltpu.VMEM((NY, NC, 2, 256, NZL * TILE), jnp.bfloat16),
            pltpu.VMEM((4, CHUNKS, q * rows, 256), jnp.float32),
            pltpu.VMEM((TILE, 128), jnp.float32),
            dma((CHUNKS,)),
            dma((CHUNKS,)),
            dma((CHUNKS,)),
            dma((CHUNKS,)),
            dma((CHUNKS,)),
            dma((CHUNKS,)),
            dma((CHUNKS,)),
            dma,
            dma((CHUNKS,)),
            dma((7,)),
            dma((7,)),
            dma((NX - 1,)),
            dma((2,)),
            dma((NY - 1,)),
            dma((NY,)),
            dma((NY,)),
            dma((NY,)),
            dma((9,)),
            dma((HEAD,)),
            dma((HEAD,)),
        ],
        compiler_params=pltpu.CompilerParams(
            collective_id=0, has_side_effects=True, vmem_limit_bytes=60 * 1024 * 1024
        ),
        cost_estimate=pl.CostEstimate(
            flops=2 * 1024 * 2048 * 1024, bytes_accessed=8 * 1024 * 1024, transcendentals=0
        ),
    )(
        amplitudes.reshape(NJ, pair_count // NJ, rows, cols),
        amplitude_map,
        integrals,
        integral_map,
        pair_list.T,
        occupied_energy,
        virtual_energy,
        virtual_energy.reshape(1, -1),
    )
    return pl.pallas_call(
        copy_out,
        out_shape=jax.ShapeDtypeStruct(amplitudes.shape, jnp.bfloat16),
        in_specs=[hbm],
        out_specs=hbm,
        scratch_shapes=[pltpu.VMEM(amplitudes.shape, jnp.bfloat16), dma((8,)), dma((8,))],
        compiler_params=pltpu.CompilerParams(vmem_limit_bytes=60 * 1024 * 1024),
    )(update)


def solution(mesh):
    in_specs = (
        P(None, "blk", "grp"),
        P("blk", "grp"),
        P("blk", None),
        P("blk", None),
        P(),
        P(),
        P(),
    )
    out_specs = P(None, "blk", "grp")
    return jax.shard_map(body, mesh=mesh, in_specs=in_specs, out_specs=out_specs, check_vma=False)
```
